256 devices in a mesh: term: 4 (over x), row: 8 (over z), col: 8 (over y, core).
Axes of the slice: x: 4, y: 4, z: 8, core: 2. Of those that a mesh axis runs over, the one named last changes fastest.
Arguments:
- coupling: bfloat16 [8, 8192, 8192], P('term', 'row', 'col'), may hold values from -0.28 to 0.28
- radial: float32 [8], replicated, may hold values from 0.5 to 1.5
- energies: float32 [8192], replicated, may hold values from 6 to 10
- labels: int32 [8192], replicated, may hold values from 0 to 11
- pivot_blocks: int32 [32], replicated, may hold values from 0 to 31, each once
- probes: float32 [8192, 512], P('col'), may hold values from -6 to 6
Outputs:
- transformed: float32 [8192, 8192], P(('row', 'term'), 'col')
- response: float32 [512, 8192], P('col', ('row', 'term'))
The draws below stay inside these ranges and needn't reach their ends.
Inputs may be any that keep to these rules, and one draw needn't show every extreme that they name: `pivot_blocks`: each of the 32 block numbers appears once; the first 2 entries are the pivot blocks in order.
All inputs are finite; a program needn't handle non-finite values.
Results may differ from the reference program's by a relative error of at most 0.0003.
Values sent between devices are 32-bit elements; how exact they have to be, the bound alone decides.
A program may use at most 64 MiB of HBM per device.

```python
import math
import jax
import jax.numpy as jnp
from jax import lax

N = 8192
TERMS = 8
PANEL = 256
PANELS = 2
LEVELS = 12
NPROBE = 512
NBLK = 32
N_TERM = 4


def draw_coupling(key, part):
    key = jax.random.fold_in(key, 11)
    scale_key, noise_key = jax.random.split(key)
    lowest = 0.5
    strength = min(0.2, 4.0 / PANEL)
    noise_part = 0.05 * jax.random.normal(noise_key, (TERMS, N, N), jnp.float32)
    profile = jax.random.uniform(scale_key, (N,), jnp.float32, lowest, 1.0)
    coherent = strength * profile[:, None] * profile[None, :]
    return jnp.clip(noise_part + coherent[None, :, :], -0.28, 0.28).astype(jnp.bfloat16)


def set_ends(entries, own_key, least, high):
    index_at = [jax.random.randint(jax.random.fold_in(own_key, axis), (), 0, length) for axis, length in enumerate(entries.shape)]
    main_axis = entries.shape.index(max(entries.shape))
    next_to = index_at[:main_axis] + [(index_at[main_axis] + 1) % entries.shape[main_axis]] + index_at[main_axis + 1:]
    return entries.at[tuple(index_at)].set(least).at[tuple(next_to)].set(high)


def block_scale(rng, extent, cuts, least, largest):
    def one(axis_at, blocks):
        draws = jax.random.uniform(jax.random.fold_in(jax.random.fold_in(rng, 6), axis_at), (blocks,), jnp.float32, least / len(cuts), largest / len(cuts))
        return jnp.repeat(jnp.exp(draws), extent[axis_at] // blocks).reshape((-1,) + (1,) * (len(extent) - axis_at - 1))

    level = one(*cuts[0])
    for cut in cuts[1:]:
        level = level * one(*cut)
    return level


def gaussian(rng, extent, width, reach, cuts=(), held_as=jnp.bfloat16):
    gain = block_scale(rng, extent, cuts, -0.22, 0.18) if cuts else 1.0
    drawn = jax.random.normal(rng, extent, jnp.float32) * width * gain
    return jnp.minimum(jnp.maximum(drawn, -reach), reach).astype(held_as)


def setup_inputs(seed: int = 0) -> dict:
    key_of = jax.random.split(jax.random.key(seed), 7)
    return {
        "coupling": draw_coupling(jax.random.fold_in(key_of[6], 71), 0),
        "radial": jnp.clip(jnp.exp(jax.random.uniform(key_of[1], (TERMS,), jnp.float32, math.log(0.5), math.log(1.5))), 0.5, 1.5),
        "energies": jnp.clip(jnp.exp(jax.random.uniform(key_of[2], (N,), jnp.float32, math.log(6.0), math.log(10.0))), 6.0, 10.0),
        "labels": set_ends(jax.random.randint(key_of[3], (N,), 0, LEVELS), jax.random.fold_in(key_of[3], 1), 0, LEVELS - 1).astype(jnp.int32),
        "pivot_blocks": jax.random.permutation(key_of[4], NBLK).astype(jnp.int32),
        "probes": gaussian(key_of[5], (N, NPROBE), 1.0, 6.0, ((0, 8),), jnp.float32),
    }


sector_step = 0.25
highest = lax.Precision.HIGHEST

def invert_pivot(pivot_block):
    normal_form = jnp.dot(pivot_block.T.astype(jnp.float32), pivot_block.astype(jnp.float32), precision=highest, preferred_element_type=jnp.float32)
    factor = jnp.linalg.cholesky(normal_form)
    return jax.scipy.linalg.cho_solve((factor, True), pivot_block.T)

def sweep_full(matrix, first_index):
    first_index = first_index.astype(jnp.int32)
    zero_index = jnp.zeros((), jnp.int32)
    pivot_rows = lax.dynamic_slice_in_dim(matrix, first_index, PANEL, 0)
    pivot_cols = lax.dynamic_slice_in_dim(matrix, first_index, PANEL, 1)
    pivot_block = lax.dynamic_slice_in_dim(pivot_rows, first_index, PANEL, 1)
    inverse = invert_pivot(pivot_block)
    new_rows = jnp.dot(inverse.astype(jnp.float32), pivot_rows.astype(jnp.float32), precision=highest, preferred_element_type=jnp.float32)
    new_rows = lax.dynamic_update_slice(new_rows, inverse, (zero_index, first_index))
    cleared = lax.dynamic_update_slice(matrix, jnp.zeros((matrix.shape[0], PANEL), jnp.float32), (zero_index, first_index))
    updated = cleared - jnp.dot(pivot_cols.astype(jnp.float32), new_rows.astype(jnp.float32), precision=highest, preferred_element_type=jnp.float32)
    return lax.dynamic_update_slice(updated, new_rows, (first_index, zero_index))

def reference(coupling, radial, energies, labels, pivot_blocks, probes):
    group_size = TERMS // N_TERM
    parity = labels % 2
    same_parity = (parity[:, None] + parity[None, :]) % 2 == 0
    even_terms = (jnp.arange(TERMS, dtype=jnp.int32) % 2 == 0).astype(jnp.float32)
    even_weight = radial * even_terms
    odd_weight = radial * (1.0 - even_terms)
    coupling_total = jnp.zeros((N, N), jnp.float32)
    for term_group in range(N_TERM):
        even_total = jnp.zeros((N, N), jnp.float32)
        odd_total = jnp.zeros((N, N), jnp.float32)
        for term_slot in range(group_size):
            term_id = term_group * group_size + term_slot
            term_layer = coupling[term_id].astype(jnp.float32)
            even_total = even_total + even_weight[term_id] * term_layer
            odd_total = odd_total + odd_weight[term_id] * term_layer
        coupling_total = coupling_total + jnp.where(same_parity, even_total, odd_total)
    matrix = sector_step * coupling_total + jnp.diag(1.0 + sector_step * energies)
    for panel_slot in range(PANELS):
        matrix = sweep_full(matrix, pivot_blocks[panel_slot] * PANEL)
    response = jnp.dot(matrix.astype(jnp.float32), probes.astype(jnp.float32), precision=highest, preferred_element_type=jnp.float32).T
    return (matrix, response)
```

```python
import functools

import jax
import jax.numpy as jnp
from jax import lax
from jax.experimental import pallas as pl
from jax.experimental.pallas import tpu as pltpu
from jax.sharding import PartitionSpec as P

MESH = pl.DeviceIdType.MESH
PANEL = 256
CHUNKS = 4
CORES = 2
F32 = jnp.float32
BF16 = jnp.bfloat16
STEP = 0.25


def aligned(index, step):
    return pl.multiple_of(index, step)


class Sends:
    def __init__(self):
        self.copies = []

    def start(self, source, target, send_sem, recv_sem, device):
        copy = pltpu.make_async_remote_copy(
            src_ref=source,
            dst_ref=target,
            send_sem=send_sem,
            recv_sem=recv_sem,
            device_id=device,
            device_id_type=MESH,
        )
        copy.start()
        self.copies.append(copy)
        return copy

    def drain(self):
        for copy in self.copies:
            copy.wait_send()
        self.copies = []


class RingReduce:
    def __init__(self, sends, device_at, pos, n, rows, own, slots, send_sem, recv_sem, source=None, stage=None):
        self.sends, self.device_at, self.pos, self.n, self.rows = sends, device_at, pos, n, rows
        self.own, self.slots, self.send_sem, self.recv_sem = own, slots, send_sem, recv_sem
        self.source, self.stage = source, stage
        self.half = rows // 2
        self.reach = n // 2
        self.sent = {}

    def neighbour(self, way):
        return self.device_at(lax.rem(self.pos + (1 if way == 0 else self.n - 1), self.n))

    def dest(self, way, distance):
        return lax.rem(self.pos + (distance if way == 0 else self.n - distance), self.n)

    def send(self, way, key, source, target):
        self.sent[way, key] = self.sends.start(
            source, target, self.send_sem.at[way, key], self.recv_sem.at[way, key], self.neighbour(way)
        )

    def start(self):
        half = self.half
        for way in range(2):
            dest = self.dest(way, self.reach)
            low = way * half
            if self.source is not None:
                source = self.source.at[pl.ds(aligned(dest * self.rows + low, half), half)]
            else:
                self.stage[way] = self.own(dest, low, half)
                source = self.stage.at[way]
            self.send(way, 0, source, self.slots.at[way, 0, pl.ds(low, half)])
        if self.source is not None:
            for way in range(2):
                dest = self.dest(way, self.reach - 1)
                other = (1 - way) * half
                source = self.source.at[pl.ds(aligned(dest * self.rows + other, half), half)]
                self.send(way, self.reach, source, self.slots.at[way, 1, pl.ds(other, half)])

    def step(self, s):
        half = self.half
        for way in range(2):
            self.sent[way, s - 1].wait_recv()
            dest = self.dest(way, self.reach - s)
            low, other = way * half, (1 - way) * half
            if s == 1:
                self.slots[way, 0, low : low + half] += self.own(dest, low, half)
                if self.source is not None:
                    part = pl.ds(low, half)
                    self.send(way, 1, self.slots.at[way, 0, part], self.slots.at[way, 1, part])
                    continue
                self.slots[way, 0, other : other + half] = self.own(dest, other, half)
            else:
                self.slots[way, s - 1] += self.own(dest, 0, self.rows)
            self.send(way, s, self.slots.at[way, s - 1], self.slots.at[way, s])

    def finish(self):
        for way in range(2):
            self.sent[way, self.reach - 1].wait_recv()
            if self.source is not None:
                self.sent[way, self.reach].wait_recv()
        last = self.reach - 1
        return self.own(self.pos, 0, self.rows) + (self.slots[0, last] + self.slots[1, last])


class RingGather:
    def __init__(self, sends, device_at, pos, n, rows, ref, base, send_sem, recv_sem):
        self.sends, self.device_at, self.pos, self.n, self.rows = sends, device_at, pos, n, rows
        self.ref, self.base, self.send_sem, self.recv_sem = ref, base, send_sem, recv_sem
        self.reach = n // 2
        self.sent = {}

    def step(self, s):
        n = self.n
        for way in range(2):
            if s > 0:
                self.sent[way, s - 1].wait_recv()
            block = lax.rem(self.pos + (n - s if way == 0 else s), n)
            to = self.device_at(lax.rem(self.pos + (1 if way == 0 else n - 1), n))
            rows = self.rows if s < self.reach - 1 else self.rows // 2
            low = 0 if s < self.reach - 1 else way * rows
            part = self.ref.at[pl.ds(aligned(self.base + block * self.rows + low, rows), rows)]
            self.sent[way, s] = self.sends.start(part, part, self.send_sem.at[way, s], self.recv_sem.at[way, s], to)

    def finish(self):
        for way in range(2):
            self.sent[way, self.reach - 1].wait_recv()


def chunk_order(pivots, col):
    first, second = pivots[0], pivots[1]
    own_first = first // CHUNKS == col
    own_second = second // CHUNKS == col
    local_first, local_second = lax.rem(first, CHUNKS), lax.rem(second, CHUNKS)
    lead = jnp.where(own_first, local_first, jnp.where(own_second, local_second, 0))
    order = [lead] + [jnp.where(lead == i, 0, i) for i in range(1, CHUNKS)]
    both = own_first & own_second
    next_up = order[1]
    for i in range(2, CHUNKS):
        order[i] = jnp.where(both & (order[i] == local_second), next_up, order[i])
    order[1] = jnp.where(both, local_second, order[1])
    return order, own_first, own_second


def exchange_kernel(
    sizes, coupling, radial, energies, labels, pivots, m0, vf, uf, af,
    qn, q, parity, x_slots, z_slots, z_stage, z_mine, z_parts, am, ac, ah, a_slots, a_mine, az, ax_mine, ax,
    um, uc, uh, u_slots,
    x_ss, x_rs, z_ss, z_rs, zx_ss, zx_rs, zg_ss, zg_rs, zy_ss, zy_rs,
    c_ss, c_rs, ay_ss, ay_rs, az_ss, az_rs, ax_ss, ax_rs, ag_ss, ag_rs, ayg_ss, ayg_rs,
    uy_ss, uy_rs, uyg_ss, uyg_rs,
):
    n_t, n_r, n_c = sizes
    n_y = n_c // CORES
    t, z, col = lax.axis_index("term"), lax.axis_index("row"), lax.axis_index("col")
    y, core = col // CORES, lax.rem(col, CORES)
    sends = Sends()

    def at_x(p):
        return {"term": p}

    def at_z(p):
        return {"row": p}

    def at_y(p):
        return {"col": p * CORES + core}

    other_core = {"col": y * CORES + (1 - core)}
    greet = [at_x(lax.rem(t + d, n_t)) for d in range(1, n_t)]
    greet += [at_z(lax.rem(z + d, n_r)) for d in range(1, n_r)]
    greet += [at_y(lax.rem(y + d, n_y)) for d in range(1, n_y)]
    greet += [other_core]
    barrier = pltpu.get_barrier_semaphore()
    for device in greet:
        pl.semaphore_signal(barrier, inc=1, device_id=device, device_id_type=MESH)

    order, own_first, own_second = chunk_order(pivots, col)
    own_both = own_first & own_second
    piv = (pivots[0], pivots[1])
    col_owned = (own_first, own_second)
    col_chunk = (jnp.int32(0), jnp.where(own_first, 1, 0))

    lab = labels[pl.ds(aligned(z * 8, 8), 8), :]
    lab = lax.rem(lab, 2).astype(F32)
    for b in range(8):
        parity[b * 128 : (b + 1) * 128, :] = jnp.broadcast_to(lab[b : b + 1, :], (128, 128)).T

    even = radial[2 * t] * STEP
    odd = radial[2 * t + 1] * STEP
    on_diagonal = jnp.where((z == col) & (t == 0), 1.0, 0.0).astype(F32)

    def fill(block):
        col_par = [lax.rem(labels[pl.ds(col * 8 + block * 2 + i, 1), :], 2).astype(F32) for i in range(2)]

        def body(b, carry):
            rows = pl.ds(aligned(b * 128, 128), 128)
            row_par = parity[rows, :]
            for i in range(2):
                cols = slice(block * PANEL + i * 128, block * PANEL + (i + 1) * 128)
                c0 = coupling[0, rows, cols].astype(F32) * even
                c1 = coupling[1, rows, cols].astype(F32) * odd
                value = jnp.where(row_par == col_par[i], c0, c1)
                qn[block, b // 2, pl.ds(aligned(lax.rem(b, 2) * 128, 128), 128), i * 128 : (i + 1) * 128] = value
            return carry

        lax.fori_loop(0, 8, body, 0)
        same = lax.broadcasted_iota(jnp.int32, (128, 128), 0) == lax.broadcasted_iota(jnp.int32, (128, 128), 1)
        for i in range(2):
            diag = (1.0 + STEP * energies[pl.ds(col * 8 + block * 2 + i, 1), :]) * on_diagonal
            part = slice(i * 128, (i + 1) * 128)
            qn[block, block, part, part] += jnp.where(same, diag, 0.0)

    def take(chunk):
        for i in range(CHUNKS):
            q[chunk, i * PANEL : (i + 1) * PANEL, :] = qn[order[chunk], i]

    def x_own(chunk):
        return lambda dest, low, n: q[chunk, pl.ds(aligned(dest * PANEL + low, 128), n), :]

    xr = [
        RingReduce(
            sends, at_x, t, n_t, PANEL, x_own(i), x_slots.at[i], x_ss.at[i], x_rs.at[i], source=q.at[i]
        )
        for i in range(CHUNKS)
    ]

    def x_finish(i):
        m0[i] = xr[i].finish()

    z_rows = 2 * PANEL // n_r

    def z_own(h):
        def load(dest, low, n):
            per = PANEL // z_rows
            which = jnp.where(dest < per, piv[0], piv[1])
            block = lax.rem(which, CHUNKS)
            rows = pl.ds(aligned(lax.rem(dest, per) * z_rows + low, 32), n)
            both = jnp.concatenate([qn[order[2 * h], block, rows, :], qn[order[2 * h + 1], block, rows, :]], axis=1)
            return jnp.where(which // CHUNKS == z, both, 0.0)

        return load

    zr = [
        RingReduce(
            sends, at_z, z, n_r, z_rows, z_own(h), z_slots.at[h], z_ss.at[h], z_rs.at[h], stage=z_stage.at[h]
        )
        for h in range(2)
    ]
    zg = [
        RingGather(sends, at_z, z, n_r, z_rows, vf.at[h], 0, zy_ss.at[h], zy_rs.at[h]) for h in range(2)
    ]
    piece = z_rows // n_t
    zx = [{}, {}]
    zxg = [{}, {}]

    def z_finish(h):
        z_mine[h] = zr[h].finish()
        for d in range(1, n_t):
            dest = lax.rem(t + d, n_t)
            zx[h][d] = sends.start(
                z_mine.at[h, pl.ds(aligned(dest * piece, piece), piece)],
                z_parts.at[h, d - 1],
                zx_ss.at[h, d - 1],
                zx_rs.at[h, d - 1],
                at_x(dest),
            )

    def z_sum(h):
        for d in range(1, n_t):
            zx[h][d].wait_recv()
        total = z_mine[h, pl.ds(aligned(t * piece, piece), piece), :]
        for d in range(1, n_t):
            total = total + z_parts[h, d - 1]
        mine = pl.ds(aligned(z * z_rows + t * piece, piece), piece)
        vf[h, mine, :] = total
        for d in range(1, n_t):
            dest = lax.rem(t + d, n_t)
            zxg[h][d] = sends.start(
                vf.at[h, mine], vf.at[h, mine], zg_ss.at[h, d - 1], zg_rs.at[h, d - 1], at_x(dest)
            )

    def z_gather(h, s):
        if s == 0:
            for d in range(1, n_t):
                zxg[h][d].wait_recv()
        zg[h].step(s)

    def a_load():
        for k in range(2):
            for l in range(2):
                mine = (piv[k] // CHUNKS == z) & col_owned[l]
                am[k * PANEL : (k + 1) * PANEL, l * PANEL : (l + 1) * PANEL] = jnp.where(
                    mine, qn[lax.rem(piv[l], CHUNKS), lax.rem(piv[k], CHUNKS)], 0.0
                )

    a_ring = RingReduce(
        sends, at_y, y, n_y, PANEL // n_y,
        lambda dest, low, n: ah[pl.ds(aligned(dest * (PANEL // n_y) + low, 32), n), :],
        a_slots, ay_ss, ay_rs, source=ah,
    )
    a_state = {}

    def a_core():
        a_load()
        a_state["core"] = sends.start(
            am.at[pl.ds(aligned((1 - core) * PANEL, PANEL), PANEL)], ac, c_ss.at[0], c_rs.at[0], other_core
        )

    def a_y0():
        a_state["core"].wait_recv()
        ah[...] = am[pl.ds(aligned(core * PANEL, PANEL), PANEL), :] + ac[...]
        a_ring.start()

    def a_y1():
        a_ring.step(1)

    a_rows = PANEL // n_y
    a_piece = a_rows // n_r

    def a_z():
        a_mine[...] = a_ring.finish()
        a_state["z"] = []
        for d in range(1, n_r):
            dest = lax.rem(z + d, n_r)
            a_state["z"].append(
                sends.start(
                    a_mine.at[pl.ds(aligned(dest * a_piece, a_piece), a_piece)],
                    az.at[d - 1],
                    az_ss.at[d - 1],
                    az_rs.at[d - 1],
                    at_z(dest),
                )
            )

    def a_x():
        for copy in a_state["z"]:
            copy.wait_recv()
        total = a_mine[pl.ds(aligned(z * a_piece, a_piece), a_piece), :]
        for d in range(1, n_r):
            total = total + az[d - 1]
        ax_mine[...] = total
        a_state["x"] = []
        for d in range(1, n_t):
            a_state["x"].append(
                sends.start(ax_mine, ax.at[d - 1], ax_ss.at[d - 1], ax_rs.at[d - 1], at_x(lax.rem(t + d, n_t)))
            )

    def a_back():
        for copy in a_state["x"]:
            copy.wait_recv()
        total = ax_mine[...]
        for d in range(1, n_t):
            total = total + ax[d - 1]
        mine = pl.ds(aligned(core * PANEL + y * a_rows + z * a_piece, a_piece), a_piece)
        af[mine, :] = total
        a_state["zg"] = [
            sends.start(
                af.at[mine], af.at[mine], ag_ss.at[d - 1], ag_rs.at[d - 1], at_z(lax.rem(z + d, n_r))
            )
            for d in range(1, n_r)
        ]

    a_gather = RingGather(sends, at_y, y, n_y, a_rows, af, core * PANEL, ayg_ss, ayg_rs)

    def a_yg0():
        for copy in a_state["zg"]:
            copy.wait_recv()
        a_gather.step(0)

    def a_yg1():
        a_gather.step(1)

    def a_core_back():
        a_gather.finish()
        part = af.at[pl.ds(aligned(core * PANEL, PANEL), PANEL)]
        a_state["core"] = sends.start(part, part, c_ss.at[1], c_rs.at[1], other_core)

    def a_done():
        a_state["core"].wait_recv()

    u_half = PANEL // CORES
    u_rows = u_half // n_y
    u_ring = RingReduce(
        sends, at_y, y, n_y, u_rows,
        lambda dest, low, n: uh[pl.ds(aligned(dest * u_rows + low, 16), n), :],
        u_slots, uy_ss, uy_rs, source=uh,
    )
    u_gather = RingGather(sends, at_y, y, n_y, u_rows, uf, core * u_half, uyg_ss, uyg_rs)
    u_state = {}

    def u_core():
        for l in range(2):
            um[:, l * PANEL : (l + 1) * PANEL] = jnp.where(col_owned[l], m0[col_chunk[l]], 0.0)
        u_state["core"] = sends.start(
            um.at[pl.ds(aligned((1 - core) * u_half, u_half), u_half)], uc, c_ss.at[2], c_rs.at[2], other_core
        )

    def u_y0():
        u_state["core"].wait_recv()
        uh[...] = um[pl.ds(aligned(core * u_half, u_half), u_half), :] + uc[...]
        u_ring.start()

    def u_y1():
        u_ring.step(1)

    def u_yg0():
        uf[pl.ds(aligned(core * u_half + y * u_rows, u_rows), u_rows), :] = u_ring.finish()
        u_gather.step(0)

    def u_yg1():
        u_gather.step(1)

    def u_core_back():
        u_gather.finish()
        part = uf.at[pl.ds(aligned(core * u_half, u_half), u_half)]
        u_state["core"] = sends.start(part, part, c_ss.at[3], c_rs.at[3], other_core)

    def u_done():
        u_state["core"].wait_recv()

    for i in range(CHUNKS):
        fill(i)
    pl.semaphore_wait(barrier, len(greet))
    a_core()
    zr[0].start()
    take(0)
    xr[0].start()
    for i in range(1, CHUNKS):
        take(i)
    a_y0()
    zr[0].step(1)
    zr[1].start()
    xr[0].step(1)
    xr[1].start()
    a_y1()
    zr[0].step(2)
    zr[1].step(1)
    a_z()
    x_finish(0)
    xr[1].step(1)
    zr[0].step(3)
    zr[1].step(2)
    a_x()
    xr[2].start()
    z_finish(0)
    zr[1].step(3)
    a_back()
    x_finish(1)
    u_core()
    z_sum(0)
    z_finish(1)
    a_yg0()
    xr[2].step(1)
    u_y0()
    z_gather(0, 0)
    z_sum(1)
    xr[3].start()
    a_yg1()
    u_y1()
    z_gather(0, 1)
    z_gather(1, 0)
    a_core_back()
    x_finish(2)
    xr[3].step(1)
    u_yg0()
    z_gather(0, 2)
    z_gather(1, 1)
    u_yg1()
    a_done()
    z_gather(0, 3)
    z_gather(1, 2)
    u_core_back()
    z_gather(1, 3)
    x_finish(3)
    u_done()
    zg[0].finish()
    zg[1].finish()
    sends.drain()


def split(value):
    high = value.astype(BF16)
    return high, (value - high.astype(F32)).astype(BF16)


def dot(a, b, dims=(((1,), (0,)), ((), ()))):
    return lax.dot_general(a, b, dims, preferred_element_type=F32)


def dot3(a, b, dims=(((1,), (0,)), ((), ()))):
    return dot(a[0], b[0], dims) + (dot(a[0], b[1], dims) + dot(a[1], b[0], dims))


def invert(af, x_ref):
    n = 2 * PANEL
    a = af[...]
    eye = jnp.where(
        lax.broadcasted_iota(jnp.int32, (n, n), 0) == lax.broadcasted_iota(jnp.int32, (n, n), 1), 1.0, 0.0
    ).astype(F32)
    size = jnp.abs(a)
    scale = 1.0 / (jnp.max(jnp.sum(size, axis=0, keepdims=True)) * jnp.max(jnp.sum(size, axis=1, keepdims=True)))
    a_high, a_low = split(a)
    x_ref[...] = a.T * scale

    def coarse(state):
        count, _ = state
        x = x_ref[...]
        x_high = x.astype(BF16)
        rest = eye - dot(a_high, x_high)
        x_ref[...] = x + dot(x_high, rest.astype(BF16))
        return count + 1, jnp.sum(rest * rest)

    _, left = lax.while_loop(lambda s: (s[0] < 24) & (s[1] > 0.1), coarse, (jnp.int32(0), jnp.float32(1e9)))

    def fine(state):
        count, _ = state
        x = x_ref[...]
        x_parts = split(x)
        rest = eye - dot3((a_high, a_low), x_parts)
        x_ref[...] = x + dot3(x_parts, split(rest))
        return count + 1, jnp.sum(rest * rest)

    start = jnp.where(left < 0.5, 0, 100).astype(jnp.int32)
    count, left = lax.while_loop(lambda s: (s[0] < 6) & (s[1] > 1e-6), fine, (start, jnp.float32(1e9)))

    def exact(a, b):
        return jnp.dot(a, b, precision=lax.Precision.HIGHEST, preferred_element_type=F32)

    @pl.when(left > 1e-6)
    def _():
        x_ref[...] = af[...].T * scale

        def full(state):
            count, _ = state
            x = x_ref[...]
            rest = eye - exact(af[...], x)
            x_ref[...] = x + exact(x, rest)
            return count + 1, jnp.sum(rest * rest)

        lax.while_loop(lambda s: (s[0] < 60) & (s[1] > 1e-7), full, (jnp.int32(0), jnp.float32(1e9)))


def update_kernel(sizes, pivots, af, uf, vf, m0, probes, out, part, x_ref, l_ref, mp):
    n_t, n_r, n_c = sizes
    t, z, col = lax.axis_index("term"), lax.axis_index("row"), lax.axis_index("col")
    group = z * n_t + t
    order, own_first, own_second = chunk_order(pivots, col)
    own_both = own_first & own_second
    invert(af, x_ref)
    inverse = split(x_ref[...])
    l_ref[...] = dot3(split(uf[...]), inverse)
    is_first, is_second = group == pivots[0], group == pivots[1]

    @pl.when(is_first)
    def _():
        l_ref[...] = -x_ref[:PANEL, :]

    @pl.when(is_second)
    def _():
        l_ref[...] = -x_ref[PANEL:, :]

    keep = jnp.where(is_first | is_second, 0.0, 1.0).astype(F32)
    left = split(l_ref[...])
    reply = jnp.zeros((PANEL, probes.shape[1]), F32)
    for chunk in range(CHUNKS):
        rows = vf[chunk // 2, :, (chunk % 2) * PANEL : (chunk % 2 + 1) * PANEL]
        value = m0[chunk] * keep - dot3(left, split(rows))
        if chunk == 0:
            value = jnp.where(
                own_first, -l_ref[:, :PANEL], jnp.where(own_second, -l_ref[:, PANEL:], value)
            )
        if chunk == 1:
            value = jnp.where(own_both, -l_ref[:, PANEL:], value)
        mp[chunk] = value
        trial = probes[pl.ds(aligned(order[chunk] * PANEL, PANEL), PANEL), :]
        reply = reply + dot3(split(value), split(trial))
    for block in range(CHUNKS):
        where = jnp.int32(0)
        for chunk in range(1, CHUNKS):
            where = jnp.where(order[chunk] == block, chunk, where)
        out[:, block * PANEL : (block + 1) * PANEL] = mp[where]
    turned = reply.T
    size = turned.shape[0] // n_c
    for j in range(n_c):
        part[j % CORES, (j // CORES) * size : (j // CORES + 1) * size, :] = turned[j * size : (j + 1) * size, :]


def response_kernel(sizes, part, out, half, arrived, slots, c_ss, c_rs, y_ss, y_rs):
    n_t, n_r, n_c = sizes
    n_y = n_c // CORES
    col = lax.axis_index("col")
    y, core = col // CORES, lax.rem(col, CORES)
    sends = Sends()

    def at_y(p):
        return {"col": p * CORES + core}

    other_core = {"col": y * CORES + (1 - core)}
    greet = [at_y(lax.rem(y + d, n_y)) for d in (1, n_y - 1)] + [other_core]
    barrier = pltpu.get_barrier_semaphore()
    for device in greet:
        pl.semaphore_signal(barrier, inc=1, device_id=device, device_id_type=MESH)
    pl.semaphore_wait(barrier, len(greet))
    copy = sends.start(part.at[1 - core], arrived, c_ss, c_rs, other_core)
    copy.wait_recv()
    half[...] = part[core] + arrived[...]
    rows = half.shape[0] // n_y
    ring = RingReduce(
        sends, at_y, y, n_y, rows,
        lambda dest, low, n: half[pl.ds(aligned(dest * rows + low, 32), n), :],
        slots, y_ss, y_rs, source=half,
    )
    ring.start()
    ring.step(1)
    out[...] = ring.finish()
    sends.drain()


VMEM = pl.BlockSpec(memory_space=pltpu.VMEM)
SMEM = pl.BlockSpec(memory_space=pltpu.SMEM)
DMA = pltpu.SemaphoreType.DMA


def on_device(sizes, coupling, radial, energies, labels, pivot_blocks, probes):
    n_t, n_r, n_c = sizes
    n_y = n_c // CORES
    tile = coupling.shape[1]
    wide = 2 * PANEL
    z_rows = wide // n_r
    f32 = lambda *shape: pltpu.VMEM(shape, F32)
    m0, vf, uf, af = pl.pallas_call(
        functools.partial(exchange_kernel, sizes),
        out_shape=(
            jax.ShapeDtypeStruct((CHUNKS, PANEL, PANEL), F32),
            jax.ShapeDtypeStruct((2, wide, wide), F32),
            jax.ShapeDtypeStruct((PANEL, wide), F32),
            jax.ShapeDtypeStruct((wide, wide), F32),
        ),
        in_specs=[VMEM, SMEM, VMEM, VMEM, SMEM],
        out_specs=(VMEM,) * 4,
        scratch_shapes=[
            f32(CHUNKS, CHUNKS, PANEL, PANEL),
            f32(CHUNKS, tile, PANEL),
            f32(tile, 128),
            f32(CHUNKS, 2, n_t // 2, PANEL, PANEL),
            f32(2, 2, n_r // 2, z_rows, wide),
            f32(2, 2, z_rows // 2, wide),
            f32(2, z_rows, wide),
            f32(2, n_t - 1, z_rows // n_t, wide),
            f32(wide, wide),
            f32(PANEL, wide),
            f32(PANEL, wide),
            f32(2, n_y // 2, PANEL // n_y, wide),
            f32(PANEL // n_y, wide),
            f32(n_r - 1, PANEL // n_y // n_r, wide),
            f32(PANEL // n_y // n_r, wide),
            f32(n_t - 1, PANEL // n_y // n_r, wide),
            f32(PANEL, wide),
            f32(PANEL // CORES, wide),
            f32(PANEL // CORES, wide),
            f32(2, n_y // 2, PANEL // CORES // n_y, wide),
            DMA((CHUNKS, 2, 3)), DMA((CHUNKS, 2, 3)),
            DMA((2, 2, n_r // 2)), DMA((2, 2, n_r // 2)),
            DMA((2, n_t - 1)), DMA((2, n_t - 1)),
            DMA((2, n_t - 1)), DMA((2, n_t - 1)),
            DMA((2, 2, n_r // 2)), DMA((2, 2, n_r // 2)),
            DMA((4,)), DMA((4,)),
            DMA((2, 3)), DMA((2, 3)),
            DMA((n_r - 1,)), DMA((n_r - 1,)),
            DMA((n_t - 1,)), DMA((n_t - 1,)),
            DMA((n_r - 1,)), DMA((n_r - 1,)),
            DMA((2, 2)), DMA((2, 2)),
            DMA((2, 3)), DMA((2, 3)),
            DMA((2, 2)), DMA((2, 2)),
        ],
        compiler_params=pltpu.CompilerParams(
            collective_id=0, has_side_effects=True, vmem_limit_bytes=48 * 1024 * 1024
        ),
        name="exchange",
    )(coupling, radial, energies.reshape(-1, 128), labels.reshape(-1, 128), pivot_blocks)
    transformed, part = pl.pallas_call(
        functools.partial(update_kernel, sizes),
        out_shape=(
            jax.ShapeDtypeStruct((PANEL, tile), F32),
            jax.ShapeDtypeStruct((CORES, probes.shape[1] // CORES, PANEL), F32),
        ),
        in_specs=[SMEM] + [VMEM] * 5,
        out_specs=(VMEM,) * 2,
        scratch_shapes=[f32(wide, wide), f32(PANEL, wide), f32(CHUNKS, PANEL, PANEL)],
        compiler_params=pltpu.CompilerParams(vmem_limit_bytes=48 * 1024 * 1024),
        name="update",
    )(pivot_blocks, af, uf, vf, m0, probes)
    width = probes.shape[1] // CORES
    response = pl.pallas_call(
        functools.partial(response_kernel, sizes),
        out_shape=jax.ShapeDtypeStruct((probes.shape[1] // n_c, PANEL), F32),
        in_specs=[VMEM],
        out_specs=VMEM,
        scratch_shapes=[
            f32(width, PANEL),
            f32(width, PANEL),
            f32(2, n_y // 2, width // n_y, PANEL),
            DMA, DMA,
            DMA((2, 3)), DMA((2, 3)),
        ],
        compiler_params=pltpu.CompilerParams(collective_id=1, has_side_effects=True),
        name="response",
    )(part)
    return transformed, response


def solution(mesh):
    sizes = tuple(mesh.shape[name] for name in ("term", "row", "col"))
    return jax.shard_map(
        functools.partial(on_device, sizes),
        mesh=mesh,
        in_specs=(P("term", "row", "col"), P(), P(), P(), P(), P("col", None)),
        out_specs=(P(("row", "term"), "col"), P("col", ("row", "term"))),
        check_vma=False,
    )
```

```python
import functools

import jax
import jax.numpy as jnp
from jax import lax
from jax.experimental import pallas as pl
from jax.experimental.pallas import tpu as pltpu
from jax.sharding import PartitionSpec as P

MESH = pl.DeviceIdType.MESH
PANEL = 256
CHUNKS = 4
CORES = 2
F32 = jnp.float32
BF16 = jnp.bfloat16
STEP = 0.25


def aligned(index, step):
    return pl.multiple_of(index, step)


class Sends:
    def __init__(self):
        self.copies = []

    def start(self, source, target, send_sem, recv_sem, device):
        copy = pltpu.make_async_remote_copy(
            src_ref=source,
            dst_ref=target,
            send_sem=send_sem,
            recv_sem=recv_sem,
            device_id=device,
            device_id_type=MESH,
        )
        copy.start()
        self.copies.append(copy)
        return copy

    def drain(self):
        for copy in self.copies:
            copy.wait_send()
        self.copies = []


class RingReduce:
    def __init__(self, sends, device_at, pos, n, rows, own, slots, send_sem, recv_sem, source=None, stage=None):
        self.sends, self.device_at, self.pos, self.n, self.rows = sends, device_at, pos, n, rows
        self.own, self.slots, self.send_sem, self.recv_sem = own, slots, send_sem, recv_sem
        self.source, self.stage = source, stage
        self.half = rows // 2
        self.reach = n // 2
        self.sent = {}

    def neighbour(self, way):
        return self.device_at(lax.rem(self.pos + (1 if way == 0 else self.n - 1), self.n))

    def dest(self, way, distance):
        return lax.rem(self.pos + (distance if way == 0 else self.n - distance), self.n)

    def send(self, way, key, source, target):
        self.sent[way, key] = self.sends.start(
            source, target, self.send_sem.at[way, key], self.recv_sem.at[way, key], self.neighbour(way)
        )

    def start(self):
        half = self.half
        for way in range(2):
            dest = self.dest(way, self.reach)
            low = way * half
            if self.source is not None:
                source = self.source.at[pl.ds(aligned(dest * self.rows + low, half), half)]
            else:
                self.stage[way] = self.own(dest, low, half)
                source = self.stage.at[way]
            self.send(way, 0, source, self.slots.at[way, 0, pl.ds(low, half)])
        if self.source is not None:
            for way in range(2):
                dest = self.dest(way, self.reach - 1)
                other = (1 - way) * half
                source = self.source.at[pl.ds(aligned(dest * self.rows + other, half), half)]
                self.send(way, self.reach, source, self.slots.at[way, 1, pl.ds(other, half)])

    def step(self, s):
        half = self.half
        for way in range(2):
            self.sent[way, s - 1].wait_recv()
            dest = self.dest(way, self.reach - s)
            low, other = way * half, (1 - way) * half
            if s == 1:
                self.slots[way, 0, low : low + half] += self.own(dest, low, half)
                if self.source is not None:
                    part = pl.ds(low, half)
                    self.send(way, 1, self.slots.at[way, 0, part], self.slots.at[way, 1, part])
                    continue
                self.slots[way, 0, other : other + half] = self.own(dest, other, half)
            else:
                self.slots[way, s - 1] += self.own(dest, 0, self.rows)
            self.send(way, s, self.slots.at[way, s - 1], self.slots.at[way, s])

    def finish(self):
        for way in range(2):
            self.sent[way, self.reach - 1].wait_recv()
            if self.source is not None:
                self.sent[way, self.reach].wait_recv()
        last = self.reach - 1
        return self.own(self.pos, 0, self.rows) + (self.slots[0, last] + self.slots[1, last])


class RingGather:
    def __init__(self, sends, device_at, pos, n, rows, ref, base, send_sem, recv_sem):
        self.sends, self.device_at, self.pos, self.n, self.rows = sends, device_at, pos, n, rows
        self.ref, self.base, self.send_sem, self.recv_sem = ref, base, send_sem, recv_sem
        self.reach = n // 2
        self.sent = {}

    def step(self, s):
        n = self.n
        for way in range(2):
            if s > 0:
                self.sent[way, s - 1].wait_recv()
            block = lax.rem(self.pos + (n - s if way == 0 else s), n)
            to = self.device_at(lax.rem(self.pos + (1 if way == 0 else n - 1), n))
            rows = self.rows if s < self.reach - 1 else self.rows // 2
            low = 0 if s < self.reach - 1 else way * rows
            part = self.ref.at[pl.ds(aligned(self.base + block * self.rows + low, rows), rows)]
            self.sent[way, s] = self.sends.start(part, part, self.send_sem.at[way, s], self.recv_sem.at[way, s], to)

    def finish(self):
        for way in range(2):
            self.sent[way, self.reach - 1].wait_recv()


def chunk_order(pivots, col):
    first, second = pivots[0], pivots[1]
    own_first = first // CHUNKS == col
    own_second = second // CHUNKS == col
    local_first, local_second = lax.rem(first, CHUNKS), lax.rem(second, CHUNKS)
    lead = jnp.where(own_first, local_first, jnp.where(own_second, local_second, 0))
    order = [lead] + [jnp.where(lead == i, 0, i) for i in range(1, CHUNKS)]
    both = own_first & own_second
    next_up = order[1]
    for i in range(2, CHUNKS):
        order[i] = jnp.where(both & (order[i] == local_second), next_up, order[i])
    order[1] = jnp.where(both, local_second, order[1])
    return order, own_first, own_second


def exchange_kernel(
    sizes, coupling_in, radial_in, energies_in, labels_in, pivots_in, probes_in,
    out, part, left_out, m0_out, vf_out, uf_out, af_out,
    coupling, radial, energies, labels, pivots, probes, p_high, p_low, m0, vf, uf, af, x_ref, a_high, a_low, l_ref, mp,
    qn, q, parity, x_slots, z_slots, z_stage, z_mine, z_parts, am, ac, ah, a_slots, a_mine, az, ax_mine, ax,
    um, uc, uh, u_slots,
    in_s, out_s,
    x_ss, x_rs, z_ss, z_rs, zx_ss, zx_rs, zg_ss, zg_rs, zy_ss, zy_rs,
    c_ss, c_rs, ay_ss, ay_rs, az_ss, az_rs, ax_ss, ax_rs, ag_ss, ag_rs, ayg_ss, ayg_rs,
    uy_ss, uy_rs, uyg_ss, uyg_rs,
):
    n_t, n_r, n_c = sizes
    n_y = n_c // CORES
    t, z, col = lax.axis_index("term"), lax.axis_index("row"), lax.axis_index("col")
    y, core = col // CORES, lax.rem(col, CORES)
    sends = Sends()
    loads = [
        pltpu.make_async_copy(source, target, in_s.at[i])
        for i, (source, target) in enumerate(
            [(pivots_in, pivots), (radial_in, radial), (labels_in, labels), (energies_in, energies)]
        )
    ]
    blocks = [
        pltpu.make_async_copy(
            coupling_in.at[:, :, pl.ds(i * PANEL, PANEL)], coupling.at[:, :, pl.ds(i * PANEL, PANEL)], in_s.at[4 + i]
        )
        for i in range(CHUNKS)
    ]
    trials = pltpu.make_async_copy(probes_in, probes, in_s.at[4 + CHUNKS])
    for copy in loads + blocks:
        copy.start()

    def at_x(p):
        return {"term": p}

    def at_z(p):
        return {"row": p}

    def at_y(p):
        return {"col": p * CORES + core}

    other_core = {"col": y * CORES + (1 - core)}
    greet = [at_x(lax.rem(t + d, n_t)) for d in range(1, n_t)]
    greet += [at_z(lax.rem(z + d, n_r)) for d in range(1, n_r)]
    greet += [at_y(lax.rem(y + d, n_y)) for d in range(1, n_y)]
    greet += [other_core]
    barrier = pltpu.get_barrier_semaphore()
    for device in greet:
        pl.semaphore_signal(barrier, inc=1, device_id=device, device_id_type=MESH)

    for copy in loads:
        copy.wait()
    order, own_first, own_second = chunk_order(pivots, col)
    own_both = own_first & own_second
    piv = (pivots[0], pivots[1])
    col_owned = (own_first, own_second)
    col_chunk = (jnp.int32(0), jnp.where(own_first, 1, 0))

    lab = labels[pl.ds(aligned(z * 8, 8), 8), :]
    lab = lax.rem(lab, 2).astype(F32)
    for b in range(8):
        parity[b * 128 : (b + 1) * 128, :] = jnp.broadcast_to(lab[b : b + 1, :], (128, 128)).T

    even = radial[2 * t] * STEP
    odd = radial[2 * t + 1] * STEP
    on_diagonal = jnp.where((z == col) & (t == 0), 1.0, 0.0).astype(F32)

    def fill(block):
        blocks[block].wait()
        col_par = [lax.rem(labels[pl.ds(col * 8 + block * 2 + i, 1), :], 2).astype(F32) for i in range(2)]

        def body(b, carry):
            rows = pl.ds(aligned(b * 128, 128), 128)
            row_par = parity[rows, :]
            for i in range(2):
                cols = slice(block * PANEL + i * 128, block * PANEL + (i + 1) * 128)
                c0 = coupling[0, rows, cols].astype(F32) * even
                c1 = coupling[1, rows, cols].astype(F32) * odd
                value = jnp.where(row_par == col_par[i], c0, c1)
                qn[block, b // 2, pl.ds(aligned(lax.rem(b, 2) * 128, 128), 128), i * 128 : (i + 1) * 128] = value
            return carry

        lax.fori_loop(0, 8, body, 0)
        same = lax.broadcasted_iota(jnp.int32, (128, 128), 0) == lax.broadcasted_iota(jnp.int32, (128, 128), 1)
        for i in range(2):
            diag = (1.0 + STEP * energies[pl.ds(col * 8 + block * 2 + i, 1), :]) * on_diagonal
            part = slice(i * 128, (i + 1) * 128)
            qn[block, block, part, part] += jnp.where(same, diag, 0.0)

    def take(chunk):
        for i in range(CHUNKS):
            q[chunk, i * PANEL : (i + 1) * PANEL, :] = qn[order[chunk], i]

    def x_own(chunk):
        return lambda dest, low, n: q[chunk, pl.ds(aligned(dest * PANEL + low, 128), n), :]

    xr = [
        RingReduce(
            sends, at_x, t, n_t, PANEL, x_own(i), x_slots.at[i], x_ss.at[i], x_rs.at[i], source=q.at[i]
        )
        for i in range(CHUNKS)
    ]

    def x_finish(i):
        m0[i] = xr[i].finish()

    z_rows = 2 * PANEL // n_r

    def z_own(h):
        def load(dest, low, n):
            per = PANEL // z_rows
            which = jnp.where(dest < per, piv[0], piv[1])
            block = lax.rem(which, CHUNKS)
            rows = pl.ds(aligned(lax.rem(dest, per) * z_rows + low, 32), n)
            return jnp.where(which // CHUNKS == z, qn[order[h], block, rows, :], 0.0)

        return load

    zr = [
        RingReduce(
            sends, at_z, z, n_r, z_rows, z_own(h), z_slots.at[h], z_ss.at[h], z_rs.at[h], stage=z_stage.at[h]
        )
        for h in range(CHUNKS)
    ]
    zg = [
        RingGather(sends, at_z, z, n_r, z_rows, vf.at[h], 0, zy_ss.at[h], zy_rs.at[h]) for h in range(CHUNKS)
    ]
    piece = z_rows // n_t
    zx = [{} for _ in range(CHUNKS)]
    zxg = [{} for _ in range(CHUNKS)]

    def z_finish(h):
        z_mine[h] = zr[h].finish()
        for d in range(1, n_t):
            dest = lax.rem(t + d, n_t)
            zx[h][d] = sends.start(
                z_mine.at[h, pl.ds(aligned(dest * piece, piece), piece)],
                z_parts.at[h, d - 1],
                zx_ss.at[h, d - 1],
                zx_rs.at[h, d - 1],
                at_x(dest),
            )

    def z_sum(h):
        for d in range(1, n_t):
            zx[h][d].wait_recv()
        total = z_mine[h, pl.ds(aligned(t * piece, piece), piece), :]
        for d in range(1, n_t):
            total = total + z_parts[h, d - 1]
        mine = pl.ds(aligned(z * z_rows + t * piece, piece), piece)
        vf[h, mine, :] = total
        for d in range(1, n_t):
            dest = lax.rem(t + d, n_t)
            zxg[h][d] = sends.start(
                vf.at[h, mine], vf.at[h, mine], zg_ss.at[h, d - 1], zg_rs.at[h, d - 1], at_x(dest)
            )

    def z_gather(h, s):
        if s == 0:
            for d in range(1, n_t):
                zxg[h][d].wait_recv()
        zg[h].step(s)

    def a_load():
        for k in range(2):
            for l in range(2):
                mine = (piv[k] // CHUNKS == z) & col_owned[l]
                am[k * PANEL : (k + 1) * PANEL, l * PANEL : (l + 1) * PANEL] = jnp.where(
                    mine, qn[lax.rem(piv[l], CHUNKS), lax.rem(piv[k], CHUNKS)], 0.0
                )

    a_ring = RingReduce(
        sends, at_y, y, n_y, PANEL // n_y,
        lambda dest, low, n: ah[pl.ds(aligned(dest * (PANEL // n_y) + low, 32), n), :],
        a_slots, ay_ss, ay_rs, source=ah,
    )
    a_state = {}

    def a_core():
        a_load()
        a_state["core"] = sends.start(
            am.at[pl.ds(aligned((1 - core) * PANEL, PANEL), PANEL)], ac, c_ss.at[0], c_rs.at[0], other_core
        )

    def a_y0():
        a_state["core"].wait_recv()
        ah[...] = am[pl.ds(aligned(core * PANEL, PANEL), PANEL), :] + ac[...]
        a_ring.start()

    def a_y1():
        a_ring.step(1)

    a_rows = PANEL // n_y
    a_piece = a_rows // n_r

    def a_z():
        a_mine[...] = a_ring.finish()
        a_state["z"] = []
        for d in range(1, n_r):
            dest = lax.rem(z + d, n_r)
            a_state["z"].append(
                sends.start(
                    a_mine.at[pl.ds(aligned(dest * a_piece, a_piece), a_piece)],
                    az.at[d - 1],
                    az_ss.at[d - 1],
                    az_rs.at[d - 1],
                    at_z(dest),
                )
            )

    def a_x():
        for copy in a_state["z"]:
            copy.wait_recv()
        total = a_mine[pl.ds(aligned(z * a_piece, a_piece), a_piece), :]
        for d in range(1, n_r):
            total = total + az[d - 1]
        ax_mine[...] = total
        ax[t] = total
        a_state["x"] = []
        for d in range(1, n_t):
            a_state["x"].append(
                sends.start(ax_mine, ax.at[t], ax_ss.at[d - 1], ax_rs.at[d - 1], at_x(lax.rem(t + d, n_t)))
            )

    def a_back():
        for copy in a_state["x"]:
            copy.wait_recv()
        total = ax[0]
        for d in range(1, n_t):
            total = total + ax[d]
        mine = pl.ds(aligned(core * PANEL + y * a_rows + z * a_piece, a_piece), a_piece)
        af[mine, :] = total
        a_state["zg"] = [
            sends.start(
                af.at[mine], af.at[mine], ag_ss.at[d - 1], ag_rs.at[d - 1], at_z(lax.rem(z + d, n_r))
            )
            for d in range(1, n_r)
        ]

    a_gather = RingGather(sends, at_y, y, n_y, a_rows, af, core * PANEL, ayg_ss, ayg_rs)

    def a_yg0():
        for copy in a_state["zg"]:
            copy.wait_recv()
        a_gather.step(0)

    def a_yg1():
        a_gather.step(1)

    def a_core_back():
        a_gather.finish()
        part = af.at[pl.ds(aligned(core * PANEL, PANEL), PANEL)]
        a_state["core"] = sends.start(part, part, c_ss.at[1], c_rs.at[1], other_core)

    def a_done():
        a_state["core"].wait_recv()

    u_half = PANEL // CORES
    u_rows = u_half // n_y
    u_ring = RingReduce(
        sends, at_y, y, n_y, u_rows,
        lambda dest, low, n: uh[pl.ds(aligned(dest * u_rows + low, 16), n), :],
        u_slots, uy_ss, uy_rs, source=uh,
    )
    u_gather = RingGather(sends, at_y, y, n_y, u_rows, uf, core * u_half, uyg_ss, uyg_rs)
    u_state = {}

    def u_core():
        for l in range(2):
            um[:, l * PANEL : (l + 1) * PANEL] = jnp.where(col_owned[l], m0[col_chunk[l]], 0.0)
        u_state["core"] = sends.start(
            um.at[pl.ds(aligned((1 - core) * u_half, u_half), u_half)], uc, c_ss.at[2], c_rs.at[2], other_core
        )

    def u_y0():
        u_state["core"].wait_recv()
        uh[...] = um[pl.ds(aligned(core * u_half, u_half), u_half), :] + uc[...]
        u_ring.start()

    def u_y1():
        u_ring.step(1)

    def u_yg0():
        uf[pl.ds(aligned(core * u_half + y * u_rows, u_rows), u_rows), :] = u_ring.finish()
        u_gather.step(0)

    def u_yg1():
        u_gather.step(1)

    def u_core_back():
        u_gather.finish()
        part = uf.at[pl.ds(aligned(core * u_half, u_half), u_half)]
        u_state["core"] = sends.start(part, part, c_ss.at[3], c_rs.at[3], other_core)

    def u_done():
        u_state["core"].wait_recv()

    n = 2 * PANEL
    eye = lambda: jnp.where(
        lax.broadcasted_iota(jnp.int32, (n, n), 0) == lax.broadcasted_iota(jnp.int32, (n, n), 1), 1.0, 0.0
    ).astype(F32)
    stores = []

    def store(source, target):
        copy = pltpu.make_async_copy(source, target, out_s.at[len(stores)])
        copy.start()
        stores.append(copy)

    def split_trials():
        trials.wait()
        for i in range(CHUNKS):
            p_high[i], p_low[i] = split(probes[i * PANEL : (i + 1) * PANEL, :])

    def inv_start():
        store(af, af_out)
        high, low = split(af[...])
        a_high[...], a_low[...] = high, low
        square = dot(high, high, (((0,), (0,)), ((), ())))
        x_ref[...] = af[...].T * (1.8 / jnp.max(jnp.sum(jnp.abs(square), axis=0, keepdims=True)))

    def coarse(count):
        def body(i, carry):
            x = x_ref[...]
            high = x.astype(BF16)
            rest = eye() - dot(a_high[...], high)
            x_ref[...] = x + dot(high, rest.astype(BF16))
            return carry

        lax.fori_loop(0, count, body, 0)

    def fine():
        x = x_ref[...]
        x_parts = split(x)
        rest = eye() - dot3((a_high[...], a_low[...]), x_parts)
        x_ref[...] = x + dot3(x_parts, split(rest))
        return jnp.sum(rest * rest)

    group = z * n_t + t
    is_first, is_second = group == piv[0], group == piv[1]
    keep = jnp.where(is_first | is_second, 0.0, 1.0).astype(F32)
    state = {}

    def inv_end():
        left_out[0] = fine()
        x = x_ref[...]
        factor = dot3(split(uf[...]), split(x))
        factor = jnp.where(is_first, -x[:PANEL, :], jnp.where(is_second, -x[PANEL:, :], factor))
        l_ref[...] = factor
        state["left"] = split(factor)

    def update(chunk):
        zg[chunk].finish()
        store(vf.at[chunk], vf_out.at[chunk])
        value = m0[chunk] * keep - dot3(state["left"], split(vf[chunk]))
        if chunk == 0:
            value = jnp.where(
                own_first, -l_ref[:, :PANEL], jnp.where(own_second, -l_ref[:, PANEL:], value)
            )
        if chunk == 1:
            value = jnp.where(own_both, -l_ref[:, PANEL:], value)
        mp[chunk] = value
        reply = dot3(split(value), (p_high[order[chunk]], p_low[order[chunk]]))
        state["reply"] = reply if chunk == 0 else state["reply"] + reply

    for i in range(CHUNKS):
        fill(i)
    pl.semaphore_wait(barrier, len(greet))
    a_core()
    zr[0].start()
    zr[1].start()
    take(0)
    xr[0].start()
    trials.start()
    for i in range(1, CHUNKS):
        take(i)
    a_y0()
    zr[0].step(1)
    zr[1].step(1)
    xr[0].step(1)
    xr[1].start()
    a_y1()
    zr[0].step(2)
    zr[1].step(2)
    zr[2].start()
    zr[3].start()
    a_z()
    x_finish(0)
    xr[1].step(1)
    zr[0].step(3)
    zr[1].step(3)
    a_x()
    zr[2].step(1)
    zr[3].step(1)
    xr[2].start()
    x_finish(1)
    u_core()
    a_back()
    z_finish(0)
    z_finish(1)
    zr[2].step(2)
    zr[3].step(2)
    a_yg0()
    u_y0()
    xr[2].step(1)
    z_sum(0)
    z_sum(1)
    zr[2].step(3)
    zr[3].step(3)
    a_yg1()
    u_y1()
    xr[3].start()
    x_finish(2)
    z_gather(0, 0)
    z_gather(1, 0)
    z_finish(2)
    z_finish(3)
    a_core_back()
    u_yg0()
    xr[3].step(1)
    split_trials()
    z_gather(0, 1)
    z_gather(1, 1)
    z_sum(2)
    z_sum(3)
    a_done()
    u_yg1()
    inv_start()
    z_gather(0, 2)
    z_gather(1, 2)
    z_gather(2, 0)
    z_gather(3, 0)
    u_core_back()
    coarse(3)
    x_finish(3)
    store(m0, m0_out)
    z_gather(0, 3)
    z_gather(1, 3)
    z_gather(2, 1)
    z_gather(3, 1)
    coarse(4)
    z_gather(2, 2)
    z_gather(3, 2)
    coarse(2)
    z_gather(2, 3)
    z_gather(3, 3)
    u_done()
    store(uf, uf_out)
    fine()
    inv_end()
    for i in range(CHUNKS):
        update(i)
    for block in range(CHUNKS):
        where = jnp.int32(0)
        for chunk in range(1, CHUNKS):
            where = jnp.where(order[chunk] == block, chunk, where)
        out[:, block * PANEL : (block + 1) * PANEL] = mp[where]
    turned = state["reply"].T
    size = turned.shape[0] // n_c
    for j in range(n_c):
        part[j % CORES, (j // CORES) * size : (j // CORES + 1) * size, :] = turned[j * size : (j + 1) * size, :]
    for copy in stores:
        copy.wait()
    sends.drain()


def split(value):
    high = value.astype(BF16)
    return high, (value - high.astype(F32)).astype(BF16)


def dot(a, b, dims=(((1,), (0,)), ((), ()))):
    return lax.dot_general(a, b, dims, preferred_element_type=F32)


def dot3(a, b, dims=(((1,), (0,)), ((), ()))):
    return dot(a[0], b[0], dims) + (dot(a[0], b[1], dims) + dot(a[1], b[0], dims))


def invert(af, x_ref):
    n = 2 * PANEL
    a = af[...]
    eye = jnp.where(
        lax.broadcasted_iota(jnp.int32, (n, n), 0) == lax.broadcasted_iota(jnp.int32, (n, n), 1), 1.0, 0.0
    ).astype(F32)
    size = jnp.abs(a)
    scale = 1.0 / (jnp.max(jnp.sum(size, axis=0, keepdims=True)) * jnp.max(jnp.sum(size, axis=1, keepdims=True)))
    a_high, a_low = split(a)
    x_ref[...] = a.T * scale

    def coarse(state):
        count, _ = state
        x = x_ref[...]
        x_high = x.astype(BF16)
        rest = eye - dot(a_high, x_high)
        x_ref[...] = x + dot(x_high, rest.astype(BF16))
        return count + 1, jnp.sum(rest * rest)

    _, left = lax.while_loop(lambda s: (s[0] < 24) & (s[1] > 0.1), coarse, (jnp.int32(0), jnp.float32(1e9)))

    def fine(state):
        count, _ = state
        x = x_ref[...]
        x_parts = split(x)
        rest = eye - dot3((a_high, a_low), x_parts)
        x_ref[...] = x + dot3(x_parts, split(rest))
        return count + 1, jnp.sum(rest * rest)

    start = jnp.where(left < 0.5, 0, 100).astype(jnp.int32)
    count, left = lax.while_loop(lambda s: (s[0] < 6) & (s[1] > 1e-6), fine, (start, jnp.float32(1e9)))

    def exact(a, b):
        return jnp.dot(a, b, precision=lax.Precision.HIGHEST, preferred_element_type=F32)

    @pl.when(left > 1e-6)
    def _():
        x_ref[...] = af[...].T * scale

        def full(state):
            count, _ = state
            x = x_ref[...]
            rest = eye - exact(af[...], x)
            x_ref[...] = x + exact(x, rest)
            return count + 1, jnp.sum(rest * rest)

        lax.while_loop(lambda s: (s[0] < 60) & (s[1] > 1e-7), full, (jnp.int32(0), jnp.float32(1e9)))


def repair_kernel(
    sizes, left, pivots, af_in, uf_in, vf_in, m0_in, probes_in, out_old, part_old, out_new, part_new,
    af, uf, vf, m0, probes, out, part, x_ref, l_ref, mp, sem,
):
    @pl.when(~(left[0] < 1e-5))
    def _():
        pairs = [(af_in, af), (uf_in, uf), (vf_in, vf), (m0_in, m0), (probes_in, probes)]
        for source, target in pairs:
            copy = pltpu.make_async_copy(source, target, sem)
            copy.start()
            copy.wait()
        n_t, n_r, n_c = sizes
        t, z, col = lax.axis_index("term"), lax.axis_index("row"), lax.axis_index("col")
        group = z * n_t + t
        order, own_first, own_second = chunk_order(pivots, col)
        own_both = own_first & own_second
        invert(af, x_ref)
        inverse = split(x_ref[...])
        l_ref[...] = dot3(split(uf[...]), inverse)
        is_first, is_second = group == pivots[0], group == pivots[1]

        @pl.when(is_first)
        def _():
            l_ref[...] = -x_ref[:PANEL, :]

        @pl.when(is_second)
        def _():
            l_ref[...] = -x_ref[PANEL:, :]

        keep = jnp.where(is_first | is_second, 0.0, 1.0).astype(F32)
        left = split(l_ref[...])
        reply = jnp.zeros((PANEL, probes.shape[1]), F32)
        for chunk in range(CHUNKS):
            rows = vf[chunk]
            value = m0[chunk] * keep - dot3(left, split(rows))
            if chunk == 0:
                value = jnp.where(
                    own_first, -l_ref[:, :PANEL], jnp.where(own_second, -l_ref[:, PANEL:], value)
                )
            if chunk == 1:
                value = jnp.where(own_both, -l_ref[:, PANEL:], value)
            mp[chunk] = value
            trial = probes[pl.ds(aligned(order[chunk] * PANEL, PANEL), PANEL), :]
            reply = reply + dot3(split(value), split(trial))
        for block in range(CHUNKS):
            where = jnp.int32(0)
            for chunk in range(1, CHUNKS):
                where = jnp.where(order[chunk] == block, chunk, where)
            out[:, block * PANEL : (block + 1) * PANEL] = mp[where]
        turned = reply.T
        size = turned.shape[0] // n_c
        for j in range(n_c):
            part[j % CORES, (j // CORES) * size : (j // CORES + 1) * size, :] = turned[j * size : (j + 1) * size, :]
        for source, target in [(out, out_new), (part, part_new)]:
            copy = pltpu.make_async_copy(source, target, sem)
            copy.start()
            copy.wait()


def response_kernel(sizes, part, out, half, arrived, slots, c_ss, c_rs, y_ss, y_rs):
    n_t, n_r, n_c = sizes
    n_y = n_c // CORES
    col = lax.axis_index("col")
    y, core = col // CORES, lax.rem(col, CORES)
    sends = Sends()

    def at_y(p):
        return {"col": p * CORES + core}

    other_core = {"col": y * CORES + (1 - core)}
    greet = [at_y(lax.rem(y + d, n_y)) for d in (1, n_y - 1)] + [other_core]
    barrier = pltpu.get_barrier_semaphore()
    for device in greet:
        pl.semaphore_signal(barrier, inc=1, device_id=device, device_id_type=MESH)
    pl.semaphore_wait(barrier, len(greet))
    copy = sends.start(part.at[1 - core], arrived, c_ss, c_rs, other_core)
    copy.wait_recv()
    half[...] = part[core] + arrived[...]
    rows = half.shape[0] // n_y
    ring = RingReduce(
        sends, at_y, y, n_y, rows,
        lambda dest, low, n: half[pl.ds(aligned(dest * rows + low, 32), n), :],
        slots, y_ss, y_rs, source=half,
    )
    ring.start()
    ring.step(1)
    out[...] = ring.finish()
    sends.drain()


VMEM = pl.BlockSpec(memory_space=pltpu.VMEM)
SMEM = pl.BlockSpec(memory_space=pltpu.SMEM)
ANY = pl.BlockSpec(memory_space=pl.ANY)
LIMIT = 63 * 1024 * 1024
DMA = pltpu.SemaphoreType.DMA


def on_device(sizes, coupling, radial, energies, labels, pivot_blocks, probes):
    n_t, n_r, n_c = sizes
    n_y = n_c // CORES
    tile = coupling.shape[1]
    wide = 2 * PANEL
    z_rows = wide // n_r
    f32 = lambda *shape: pltpu.VMEM(shape, F32)
    width = probes.shape[1] // CORES
    shape = lambda *dims: jax.ShapeDtypeStruct(dims, F32)
    i32 = lambda *dims: pltpu.VMEM(dims, jnp.int32)
    bf16 = lambda *dims: pltpu.VMEM(dims, BF16)
    count = probes.shape[1]
    out, part, left, m0, vf, uf, af = pl.pallas_call(
        functools.partial(exchange_kernel, sizes),
        out_shape=(
            shape(PANEL, tile),
            shape(CORES, width, PANEL),
            shape(1),
            shape(CHUNKS, PANEL, PANEL),
            shape(CHUNKS, wide, PANEL),
            shape(PANEL, wide),
            shape(wide, wide),
        ),
        in_specs=[ANY] * 6,
        out_specs=(VMEM, VMEM, SMEM) + (ANY,) * 4,
        scratch_shapes=[
            bf16(*coupling.shape),
            pltpu.SMEM(radial.shape, F32),
            f32(energies.shape[0] // 128, 128),
            i32(labels.shape[0] // 128, 128),
            pltpu.SMEM(pivot_blocks.shape, jnp.int32),
            f32(*probes.shape),
            bf16(CHUNKS, PANEL, count),
            bf16(CHUNKS, PANEL, count),
            f32(CHUNKS, PANEL, PANEL),
            f32(CHUNKS, wide, PANEL),
            f32(PANEL, wide),
            f32(wide, wide),
            f32(wide, wide),
            bf16(wide, wide),
            bf16(wide, wide),
            f32(PANEL, wide),
            f32(CHUNKS, PANEL, PANEL),
            f32(CHUNKS, CHUNKS, PANEL, PANEL),
            f32(CHUNKS, tile, PANEL),
            f32(tile, 128),
            f32(CHUNKS, 2, n_t // 2, PANEL, PANEL),
            f32(CHUNKS, 2, n_r // 2, z_rows, PANEL),
            f32(CHUNKS, 2, z_rows // 2, PANEL),
            f32(CHUNKS, z_rows, PANEL),
            f32(CHUNKS, n_t - 1, z_rows // n_t, PANEL),
            f32(wide, wide),
            f32(PANEL, wide),
            f32(PANEL, wide),
            f32(2, n_y // 2, PANEL // n_y, wide),
            f32(PANEL // n_y, wide),
            f32(n_r - 1, PANEL // n_y // n_r, wide),
            f32(PANEL // n_y // n_r, wide),
            f32(n_t, PANEL // n_y // n_r, wide),
            f32(PANEL, wide),
            f32(PANEL // CORES, wide),
            f32(PANEL // CORES, wide),
            f32(2, n_y // 2, PANEL // CORES // n_y, wide),
            DMA((5 + CHUNKS,)), DMA((3 + CHUNKS,)),
            DMA((CHUNKS, 2, 3)), DMA((CHUNKS, 2, 3)),
            DMA((CHUNKS, 2, n_r // 2)), DMA((CHUNKS, 2, n_r // 2)),
            DMA((CHUNKS, n_t - 1)), DMA((CHUNKS, n_t - 1)),
            DMA((CHUNKS, n_t - 1)), DMA((CHUNKS, n_t - 1)),
            DMA((CHUNKS, 2, n_r // 2)), DMA((CHUNKS, 2, n_r // 2)),
            DMA((4,)), DMA((4,)),
            DMA((2, 3)), DMA((2, 3)),
            DMA((n_r - 1,)), DMA((n_r - 1,)),
            DMA((n_t - 1,)), DMA((n_t - 1,)),
            DMA((n_r - 1,)), DMA((n_r - 1,)),
            DMA((2, 2)), DMA((2, 2)),
            DMA((2, 3)), DMA((2, 3)),
            DMA((2, 2)), DMA((2, 2)),
        ],
        compiler_params=pltpu.CompilerParams(
            collective_id=0, has_side_effects=True, vmem_limit_bytes=LIMIT
        ),
        name="exchange",
    )(coupling, radial, energies.reshape(-1, 128), labels.reshape(-1, 128), pivot_blocks, probes)
    transformed, part = pl.pallas_call(
        functools.partial(repair_kernel, sizes),
        out_shape=(shape(PANEL, tile), shape(CORES, width, PANEL)),
        in_specs=[SMEM, SMEM] + [ANY] * 7,
        out_specs=(ANY, ANY),
        input_output_aliases={7: 0, 8: 1},
        scratch_shapes=[
            f32(wide, wide), f32(PANEL, wide), f32(CHUNKS, wide, PANEL), f32(CHUNKS, PANEL, PANEL),
            f32(*probes.shape), f32(PANEL, tile), f32(CORES, width, PANEL),
            f32(wide, wide), f32(PANEL, wide), f32(CHUNKS, PANEL, PANEL), DMA,
        ],
        compiler_params=pltpu.CompilerParams(vmem_limit_bytes=LIMIT),
        name="repair",
    )(left, pivot_blocks, af, uf, vf, m0, probes, out, part)
    response = pl.pallas_call(
        functools.partial(response_kernel, sizes),
        out_shape=jax.ShapeDtypeStruct((probes.shape[1] // n_c, PANEL), F32),
        in_specs=[VMEM],
        out_specs=VMEM,
        scratch_shapes=[
            f32(width, PANEL),
            f32(width, PANEL),
            f32(2, n_y // 2, width // n_y, PANEL),
            DMA, DMA,
            DMA((2, 3)), DMA((2, 3)),
        ],
        compiler_params=pltpu.CompilerParams(collective_id=1, has_side_effects=True),
        name="response",
    )(part)
    return transformed, response


def solution(mesh):
    sizes = tuple(mesh.shape[name] for name in ("term", "row", "col"))
    return jax.shard_map(
        functools.partial(on_device, sizes),
        mesh=mesh,
        in_specs=(P("term", "row", "col"), P(), P(), P(), P(), P("col", None)),
        out_specs=(P(("row", "term"), "col"), P("col", ("row", "term"))),
        check_vma=False,
    )
```

```python
import functools

import jax
import jax.numpy as jnp
from jax import lax
from jax.experimental import pallas as pl
from jax.experimental.pallas import tpu as pltpu
from jax.sharding import PartitionSpec as P

MESH = pl.DeviceIdType.MESH
PANEL = 256
CHUNKS = 4
CORES = 2
F32 = jnp.float32
BF16 = jnp.bfloat16
STEP = 0.25


def aligned(index, step):
    return pl.multiple_of(index, step)


class Sends:
    def __init__(self):
        self.copies = []

    def start(self, source, target, send_sem, recv_sem, device):
        copy = pltpu.make_async_remote_copy(
            src_ref=source,
            dst_ref=target,
            send_sem=send_sem,
            recv_sem=recv_sem,
            device_id=device,
            device_id_type=MESH,
        )
        copy.start()
        self.copies.append(copy)
        return copy

    def drain(self):
        for copy in self.copies:
            copy.wait_send()
        self.copies = []


class RingReduce:
    def __init__(self, sends, device_at, pos, n, rows, own, slots, send_sem, recv_sem, source=None, stage=None):
        self.sends, self.device_at, self.pos, self.n, self.rows = sends, device_at, pos, n, rows
        self.own, self.slots, self.send_sem, self.recv_sem = own, slots, send_sem, recv_sem
        self.source, self.stage = source, stage
        self.half = rows // 2
        self.reach = n // 2
        self.sent = {}

    def neighbour(self, way):
        return self.device_at(lax.rem(self.pos + (1 if way == 0 else self.n - 1), self.n))

    def dest(self, way, distance):
        return lax.rem(self.pos + (distance if way == 0 else self.n - distance), self.n)

    def send(self, way, key, source, target):
        self.sent[way, key] = self.sends.start(
            source, target, self.send_sem.at[way, key], self.recv_sem.at[way, key], self.neighbour(way)
        )

    def start(self):
        half = self.half
        for way in range(2):
            dest = self.dest(way, self.reach)
            low = way * half
            if self.source is not None:
                source = self.source.at[pl.ds(aligned(dest * self.rows + low, half), half)]
            else:
                self.stage[way] = self.own(dest, low, half)
                source = self.stage.at[way]
            self.send(way, 0, source, self.slots.at[way, 0, pl.ds(low, half)])
        if self.source is not None:
            for way in range(2):
                dest = self.dest(way, self.reach - 1)
                other = (1 - way) * half
                source = self.source.at[pl.ds(aligned(dest * self.rows + other, half), half)]
                self.send(way, self.reach, source, self.slots.at[way, 1, pl.ds(other, half)])

    def step(self, s):
        half = self.half
        for way in range(2):
            self.sent[way, s - 1].wait_recv()
            dest = self.dest(way, self.reach - s)
            low, other = way * half, (1 - way) * half
            if s == 1:
                self.slots[way, 0, low : low + half] += self.own(dest, low, half)
                if self.source is not None:
                    part = pl.ds(low, half)
                    self.send(way, 1, self.slots.at[way, 0, part], self.slots.at[way, 1, part])
                    continue
                self.slots[way, 0, other : other + half] = self.own(dest, other, half)
            else:
                self.slots[way, s - 1] += self.own(dest, 0, self.rows)
            self.send(way, s, self.slots.at[way, s - 1], self.slots.at[way, s])

    def finish(self):
        for way in range(2):
            self.sent[way, self.reach - 1].wait_recv()
            if self.source is not None:
                self.sent[way, self.reach].wait_recv()
        last = self.reach - 1
        return self.own(self.pos, 0, self.rows) + (self.slots[0, last] + self.slots[1, last])


class RingGather:
    def __init__(self, sends, device_at, pos, n, rows, ref, base, send_sem, recv_sem):
        self.sends, self.device_at, self.pos, self.n, self.rows = sends, device_at, pos, n, rows
        self.ref, self.base, self.send_sem, self.recv_sem = ref, base, send_sem, recv_sem
        self.reach = n // 2
        self.sent = {}

    def step(self, s):
        n = self.n
        for way in range(2):
            if s > 0:
                self.sent[way, s - 1].wait_recv()
            block = lax.rem(self.pos + (n - s if way == 0 else s), n)
            to = self.device_at(lax.rem(self.pos + (1 if way == 0 else n - 1), n))
            rows = self.rows if s < self.reach - 1 else self.rows // 2
            low = 0 if s < self.reach - 1 else way * rows
            part = self.ref.at[pl.ds(aligned(self.base + block * self.rows + low, rows), rows)]
            self.sent[way, s] = self.sends.start(part, part, self.send_sem.at[way, s], self.recv_sem.at[way, s], to)

    def finish(self):
        for way in range(2):
            self.sent[way, self.reach - 1].wait_recv()


def chunk_order(pivots, col):
    first, second = pivots[0], pivots[1]
    own_first = first // CHUNKS == col
    own_second = second // CHUNKS == col
    local_first, local_second = lax.rem(first, CHUNKS), lax.rem(second, CHUNKS)
    lead = jnp.where(own_first, local_first, jnp.where(own_second, local_second, 0))
    order = [lead] + [jnp.where(lead == i, 0, i) for i in range(1, CHUNKS)]
    both = own_first & own_second
    next_up = order[1]
    for i in range(2, CHUNKS):
        order[i] = jnp.where(both & (order[i] == local_second), next_up, order[i])
    order[1] = jnp.where(both, local_second, order[1])
    return order, own_first, own_second


def exchange_kernel(
    sizes, coupling_in, radial_in, energies_in, labels_in, pivots_in, probes_in,
    out, answer, left_out, m0_out, vf_out, uf_out, af_out, r0, w,
    coupling, radial, energies, labels, pivots, probes, p_high, p_low, m0, vf, uf, af, x_ref, a_high, a_low, l_ref, mp,
    vsrc, qn, q, parity, x_slots, z_slots, z_stage, z_mine, z_parts, am, ac, ah, a_slots, a_mine, az, ax_mine, ax,
    um, uc, uh, u_slots, reply, part, r_half, r_got, r_slots, w_mine, w_slots, w_all,
    in_s, out_s,
    x_ss, x_rs, z_ss, z_rs, zx_ss, zx_rs, zg_ss, zg_rs, zy_ss, zy_rs,
    c_ss, c_rs, ay_ss, ay_rs, az_ss, az_rs, ax_ss, ax_rs, ag_ss, ag_rs, ayg_ss, ayg_rs,
    uy_ss, uy_rs, uyg_ss, uyg_rs, ry_ss, ry_rs, wc_ss, wc_rs, wz_ss, wz_rs, wx_ss, wx_rs,
):
    n_t, n_r, n_c = sizes
    n_y = n_c // CORES
    t, z, col = lax.axis_index("term"), lax.axis_index("row"), lax.axis_index("col")
    y, core = col // CORES, lax.rem(col, CORES)
    sends = Sends()
    loads = [
        pltpu.make_async_copy(source, target, in_s.at[i])
        for i, (source, target) in enumerate(
            [(pivots_in, pivots), (radial_in, radial), (labels_in, labels), (energies_in, energies)]
        )
    ]
    blocks = [
        pltpu.make_async_copy(
            coupling_in.at[:, pl.ds(i * PANEL, PANEL)], coupling.at[:, i], in_s.at[4 + i]
        )
        for i in range(CHUNKS)
    ]
    trials = pltpu.make_async_copy(probes_in, probes, in_s.at[4 + CHUNKS])
    for copy in loads + blocks:
        copy.start()

    def at_x(p):
        return {"term": p}

    def at_z(p):
        return {"row": p}

    def at_y(p):
        return {"col": p * CORES + core}

    other_core = {"col": y * CORES + (1 - core)}
    greet = [at_x(lax.rem(t + d, n_t)) for d in range(1, n_t)]
    greet += [at_z(lax.rem(z + d, n_r)) for d in range(1, n_r)]
    greet += [{"col": lax.rem(col + d, n_c)} for d in range(1, n_c)]
    barrier = pltpu.get_barrier_semaphore()
    for device in greet:
        pl.semaphore_signal(barrier, inc=1, device_id=device, device_id_type=MESH)

    for copy in loads:
        copy.wait()
    order, own_first, own_second = chunk_order(pivots, col)
    own_both = own_first & own_second
    piv = (pivots[0], pivots[1])
    col_owned = (own_first, own_second)
    col_chunk = (jnp.int32(0), jnp.where(own_first, 1, 0))

    lab = labels[pl.ds(aligned(z * 8, 8), 8), :]
    lab = lax.rem(lab, 2).astype(F32)
    for b in range(8):
        parity[b] = jnp.broadcast_to(lab[b : b + 1, :], (128, 128)).T

    even = radial[2 * t] * STEP
    odd = radial[2 * t + 1] * STEP
    on_diagonal = jnp.where((z == col) & (t == 0), 1.0, 0.0).astype(F32)

    def column_rows(table, block):
        return [table[pl.ds(col * 8 + block * 2 + i, 1), :] for i in range(2)]

    def layers(group, half, rows, block, col_par, i):
        cols = slice(block * PANEL + i * 128, block * PANEL + (i + 1) * 128)
        c0 = coupling[0, group, rows, cols].astype(F32) * even
        c1 = coupling[1, group, rows, cols].astype(F32) * odd
        return jnp.where(parity[group * 2 + half] == col_par[i], c0, c1)

    same = lax.broadcasted_iota(jnp.int32, (128, 128), 0) == lax.broadcasted_iota(jnp.int32, (128, 128), 1)

    def fill_pivot(k):
        group = lax.rem(piv[k], CHUNKS)
        mine = piv[k] // CHUNKS == z
        for block in range(CHUNKS):
            col_par = [lax.rem(v, 2).astype(F32) for v in column_rows(labels, block)]
            diag = [(1.0 + STEP * v) * on_diagonal for v in column_rows(energies, block)]
            for half in range(2):
                rows = slice(half * 128, (half + 1) * 128)
                for i in range(2):
                    value = layers(group, half, rows, block, col_par, i)
                    if i == half:
                        value = value + jnp.where(same & (group == block), diag[i], 0.0)
                    vsrc[k, block, rows, i * 128 : (i + 1) * 128] = jnp.where(mine, value, 0.0)

    def fill(block):
        col_par = [lax.rem(v, 2).astype(F32) for v in column_rows(labels, block)]

        def body(group, carry):
            for half in range(2):
                rows = slice(half * 128, (half + 1) * 128)
                for i in range(2):
                    qn[block, group, rows, i * 128 : (i + 1) * 128] = layers(group, half, rows, block, col_par, i)
            return carry

        lax.fori_loop(0, CHUNKS, body, 0)
        for i, v in enumerate(column_rows(energies, block)):
            part = slice(i * 128, (i + 1) * 128)
            qn[block, block, part, part] += jnp.where(same, (1.0 + STEP * v) * on_diagonal, 0.0)

    def take(chunk):
        for i in range(CHUNKS):
            q[chunk, i * PANEL : (i + 1) * PANEL, :] = qn[order[chunk], i]

    def x_own(chunk):
        return lambda dest, low, n: q[chunk, pl.ds(aligned(dest * PANEL + low, 128), n), :]

    xr = [
        RingReduce(
            sends, at_x, t, n_t, PANEL, x_own(i), x_slots.at[i], x_ss.at[i], x_rs.at[i], source=q.at[i]
        )
        for i in range(CHUNKS)
    ]

    def x_finish(i):
        m0[i] = xr[i].finish()

    z_rows = 2 * PANEL // n_r

    def z_own(h):
        def load(dest, low, n):
            per = PANEL // z_rows
            which = jnp.where(dest < per, 0, 1)
            return vsrc[which, h, pl.ds(aligned(lax.rem(dest, per) * z_rows + low, 32), n), :]

        return load

    zr = [
        RingReduce(
            sends, at_z, z, n_r, z_rows, z_own(h), z_slots.at[h], z_ss.at[h], z_rs.at[h], stage=z_stage.at[h]
        )
        for h in range(CHUNKS)
    ]
    zg = [
        RingGather(sends, at_z, z, n_r, z_rows, vf.at[h], 0, zy_ss.at[h], zy_rs.at[h]) for h in range(CHUNKS)
    ]
    piece = z_rows // n_t
    zx = [{} for _ in range(CHUNKS)]
    zxg = [{} for _ in range(CHUNKS)]

    def z_finish(h):
        z_mine[h] = zr[h].finish()
        for d in range(1, n_t):
            dest = lax.rem(t + d, n_t)
            zx[h][d] = sends.start(
                z_mine.at[h, pl.ds(aligned(dest * piece, piece), piece)],
                z_parts.at[h, d - 1],
                zx_ss.at[h, d - 1],
                zx_rs.at[h, d - 1],
                at_x(dest),
            )

    def z_sum(h):
        for d in range(1, n_t):
            zx[h][d].wait_recv()
        total = z_mine[h, pl.ds(aligned(t * piece, piece), piece), :]
        for d in range(1, n_t):
            total = total + z_parts[h, d - 1]
        mine = pl.ds(aligned(z * z_rows + t * piece, piece), piece)
        vf[h, mine, :] = total
        for d in range(1, n_t):
            dest = lax.rem(t + d, n_t)
            zxg[h][d] = sends.start(
                vf.at[h, mine], vf.at[h, mine], zg_ss.at[h, d - 1], zg_rs.at[h, d - 1], at_x(dest)
            )

    def z_gather(h, s):
        if s == 0:
            for d in range(1, n_t):
                zxg[h][d].wait_recv()
        zg[h].step(s)

    def a_load():
        for k in range(2):
            for l in range(2):
                am[k * PANEL : (k + 1) * PANEL, l * PANEL : (l + 1) * PANEL] = jnp.where(
                    col_owned[l], vsrc[k, lax.rem(piv[l], CHUNKS)], 0.0
                )

    a_ring = RingReduce(
        sends, at_y, y, n_y, PANEL // n_y,
        lambda dest, low, n: ah[pl.ds(aligned(dest * (PANEL // n_y) + low, 32), n), :],
        a_slots, ay_ss, ay_rs, source=ah,
    )
    a_state = {}

    def a_core():
        a_load()
        a_state["core"] = sends.start(
            am.at[pl.ds(aligned((1 - core) * PANEL, PANEL), PANEL)], ac, c_ss.at[0], c_rs.at[0], other_core
        )

    def a_y0():
        a_state["core"].wait_recv()
        ah[...] = am[pl.ds(aligned(core * PANEL, PANEL), PANEL), :] + ac[...]
        a_ring.start()

    def a_y1():
        a_ring.step(1)

    a_rows = PANEL // n_y
    a_piece = a_rows // n_r

    def a_z():
        a_mine[...] = a_ring.finish()
        a_state["z"] = []
        for d in range(1, n_r):
            dest = lax.rem(z + d, n_r)
            a_state["z"].append(
                sends.start(
                    a_mine.at[pl.ds(aligned(dest * a_piece, a_piece), a_piece)],
                    az.at[d - 1],
                    az_ss.at[d - 1],
                    az_rs.at[d - 1],
                    at_z(dest),
                )
            )

    def a_x():
        for copy in a_state["z"]:
            copy.wait_recv()
        total = a_mine[pl.ds(aligned(z * a_piece, a_piece), a_piece), :]
        for d in range(1, n_r):
            total = total + az[d - 1]
        ax_mine[...] = total
        ax[t] = total
        a_state["x"] = []
        for d in range(1, n_t):
            a_state["x"].append(
                sends.start(ax_mine, ax.at[t], ax_ss.at[d - 1], ax_rs.at[d - 1], at_x(lax.rem(t + d, n_t)))
            )

    def a_back():
        for copy in a_state["x"]:
            copy.wait_recv()
        total = ax[0]
        for d in range(1, n_t):
            total = total + ax[d]
        mine = pl.ds(aligned(core * PANEL + y * a_rows + z * a_piece, a_piece), a_piece)
        af[mine, :] = total
        a_state["zg"] = [
            sends.start(
                af.at[mine], af.at[mine], ag_ss.at[d - 1], ag_rs.at[d - 1], at_z(lax.rem(z + d, n_r))
            )
            for d in range(1, n_r)
        ]

    a_gather = RingGather(sends, at_y, y, n_y, a_rows, af, core * PANEL, ayg_ss, ayg_rs)

    def a_yg0():
        for copy in a_state["zg"]:
            copy.wait_recv()
        a_gather.step(0)

    def a_yg1():
        a_gather.step(1)

    def a_core_back():
        a_gather.finish()
        part = af.at[pl.ds(aligned(core * PANEL, PANEL), PANEL)]
        a_state["core"] = sends.start(part, part, c_ss.at[1], c_rs.at[1], other_core)

    def a_done():
        a_state["core"].wait_recv()

    u_half = PANEL // CORES
    u_rows = u_half // n_y
    u_ring = RingReduce(
        sends, at_y, y, n_y, u_rows,
        lambda dest, low, n: uh[pl.ds(aligned(dest * u_rows + low, 16), n), :],
        u_slots, uy_ss, uy_rs, source=uh,
    )
    u_gather = RingGather(sends, at_y, y, n_y, u_rows, uf, core * u_half, uyg_ss, uyg_rs)
    u_state = {}

    def u_core():
        for l in range(2):
            um[:, l * PANEL : (l + 1) * PANEL] = jnp.where(col_owned[l], m0[col_chunk[l]], 0.0)
        u_state["core"] = sends.start(
            um.at[pl.ds(aligned((1 - core) * u_half, u_half), u_half)], uc, c_ss.at[2], c_rs.at[2], other_core
        )

    def u_y0():
        u_state["core"].wait_recv()
        uh[...] = um[pl.ds(aligned(core * u_half, u_half), u_half), :] + uc[...]
        u_ring.start()

    def u_y1():
        u_ring.step(1)

    def u_yg0():
        uf[pl.ds(aligned(core * u_half + y * u_rows, u_rows), u_rows), :] = u_ring.finish()
        u_gather.step(0)

    def u_yg1():
        u_gather.step(1)

    def u_core_back():
        u_gather.finish()
        part = uf.at[pl.ds(aligned(core * u_half, u_half), u_half)]
        u_state["core"] = sends.start(part, part, c_ss.at[3], c_rs.at[3], other_core)

    def u_done():
        u_state["core"].wait_recv()

    n = 2 * PANEL
    eye = lambda: jnp.where(
        lax.broadcasted_iota(jnp.int32, (n, n), 0) == lax.broadcasted_iota(jnp.int32, (n, n), 1), 1.0, 0.0
    ).astype(F32)
    stores = []

    def store(source, target):
        copy = pltpu.make_async_copy(source, target, out_s.at[len(stores)])
        copy.start()
        stores.append(copy)

    def split_trials():
        trials.wait()
        for i in range(CHUNKS):
            p_high[i], p_low[i] = split(probes[i * PANEL : (i + 1) * PANEL, :])

    def inv_start():
        store(af, af_out)
        high, low = split(af[...])
        a_high[...], a_low[...] = high, low
        square = dot(high, high, (((0,), (0,)), ((), ())))
        x_ref[...] = af[...].T * (1.8 / jnp.max(jnp.sum(jnp.abs(square), axis=0, keepdims=True)))

    def coarse(count):
        def body(i, carry):
            x = x_ref[...]
            high = x.astype(BF16)
            rest = eye() - dot(a_high[...], high)
            x_ref[...] = x + dot(high, rest.astype(BF16))
            return carry

        lax.fori_loop(0, count, body, 0)

    def fine():
        x = x_ref[...]
        x_parts = split(x)
        rest = eye() - dot3((a_high[...], a_low[...]), x_parts)
        x_ref[...] = x + dot3(x_parts, split(rest))
        return jnp.sum(rest * rest)

    group = z * n_t + t
    is_first, is_second = group == piv[0], group == piv[1]
    keep = jnp.where(is_first | is_second, 0.0, 1.0).astype(F32)
    state = {}

    def inv_end():
        left_out[0] = fine()
        x = x_ref[...]
        factor = dot3(split(uf[...]), split(x))
        factor = jnp.where(is_first, -x[:PANEL, :], jnp.where(is_second, -x[PANEL:, :], factor))
        l_ref[...] = factor
        state["left"] = split(factor)

    def update(chunk):
        value = m0[chunk] * keep - dot3(state["left"], split(vf[order[chunk]]))
        if chunk == 0:
            value = jnp.where(
                own_first, -l_ref[:, :PANEL], jnp.where(own_second, -l_ref[:, PANEL:], value)
            )
        if chunk == 1:
            value = jnp.where(own_both, -l_ref[:, PANEL:], value)
        mp[chunk] = value

    def r_add(chunk):
        factor = keep
        if chunk == 0:
            factor = jnp.where(own_first | own_second, 0.0, keep)
        if chunk == 1:
            factor = jnp.where(own_both, 0.0, keep)
        add = dot3(split(m0[chunk] * factor), (p_high[order[chunk]], p_low[order[chunk]]))
        if chunk == 0:
            reply[...] = add
        else:
            reply[...] += add

    r_rows = part.shape[1] // n_y
    r_ring = RingReduce(
        sends, at_y, y, n_y, r_rows,
        lambda dest, low, n: r_half[pl.ds(aligned(dest * r_rows + low, 32), n), :],
        r_slots, ry_ss, ry_rs, source=r_half,
    )

    def r_core():
        turned = reply[...].T
        for j in range(n_c):
            part[j % CORES, (j // CORES) * r_rows : (j // CORES + 1) * r_rows, :] = turned[
                j * r_rows : (j + 1) * r_rows, :
            ]
        state["r"] = sends.start(part.at[1 - core], r_got, c_ss.at[4], c_rs.at[4], other_core)

    def r_y0():
        state["r"].wait_recv()
        r_half[...] = part[core] + r_got[...]
        r_ring.start()

    def r_y1():
        r_ring.step(1)

    def r_done():
        r0[...] = r_ring.finish()

    lanes = w_mine.shape[2]

    def w_cols():
        first = z * z_rows + t * piece
        row_id = lax.broadcasted_iota(jnp.int32, (piece, PANEL), 0) + first
        col_id = lax.broadcasted_iota(jnp.int32, (piece, PANEL), 1)
        total = jnp.zeros((piece, probes.shape[1]), F32)
        for h in range(CHUNKS):
            value = vf[h, pl.ds(aligned(first, piece), piece), :]
            for l in range(2):
                here = col_owned[l] & (lax.rem(piv[l], CHUNKS) == h)
                unit = jnp.where(row_id == col_id + l * PANEL, 1.0, 0.0).astype(F32)
                value = jnp.where(here, unit, value)
            total = total + dot3(split(value), (p_high[h], p_low[h]))
        for i in range(n_y):
            w_mine[i] = total[:, i * lanes : (i + 1) * lanes]
        state["wc"] = []
        for d in range(1, n_c):
            dest = lax.rem(col + d, n_c)
            state["wc"].append(
                sends.start(
                    w_mine.at[dest // CORES], w_slots.at[d - 1], wc_ss.at[d - 1], wc_rs.at[d - 1], {"col": dest}
                )
            )

    def w_z():
        total = w_mine[y]
        for d in range(1, n_c):
            state["wc"][d - 1].wait_recv()
            total = total + w_slots[d - 1]
        mine = pl.ds(aligned(z * piece, piece), piece)
        w_all[t, mine, :] = total
        state["wz"] = [
            sends.start(
                w_all.at[t, mine], w_all.at[t, mine], wz_ss.at[d - 1], wz_rs.at[d - 1], at_z(lax.rem(z + d, n_r))
            )
            for d in range(1, n_r)
        ]

    def w_x():
        for copy in state["wz"]:
            copy.wait_recv()
        state["wx"] = [
            sends.start(w_all.at[t], w_all.at[t], wx_ss.at[d - 1], wx_rs.at[d - 1], at_x(lax.rem(t + d, n_t)))
            for d in range(1, n_t)
        ]

    def w_done():
        for copy in state["wx"]:
            copy.wait_recv()
        for i in range(n_t):
            for j in range(n_r):
                first = j * z_rows + i * piece
                w[first : first + piece, :] = w_all[i, j * piece : (j + 1) * piece, :]

    def respond():
        both = dot3(state["left"], split(w[...])).T
        answer[...] = r0[...] - jnp.where(core == 0, both[:r_rows], both[r_rows:])

    for copy in blocks:
        copy.wait()
    fill_pivot(0)
    fill_pivot(1)
    pl.semaphore_wait(barrier, len(greet))
    for i in range(CHUNKS):
        zr[i].start()
    a_core()
    trials.start()
    for i in range(CHUNKS):
        fill(i)
    take(0)
    xr[0].start()
    for i in range(CHUNKS):
        zr[i].step(1)
    a_y0()
    take(1)
    take(2)
    take(3)
    for i in (0, 1):
        zr[i].step(2)
    xr[0].step(1)
    xr[1].start()
    a_y1()
    for i in (2, 3):
        zr[i].step(2)
    split_trials()
    a_z()
    for i in (0, 1):
        zr[i].step(3)
    x_finish(0)
    a_x()
    for i in (2, 3):
        zr[i].step(3)
    xr[1].step(1)
    xr[2].start()
    a_back()
    for i in (0, 1):
        z_finish(i)
    a_yg0()
    for i in (2, 3):
        z_finish(i)
    x_finish(1)
    u_core()
    r_add(0)
    r_add(1)
    for i in (0, 1):
        z_sum(i)
    a_yg1()
    for i in (2, 3):
        z_sum(i)
    xr[2].step(1)
    xr[3].start()
    u_y0()
    for i in (0, 1):
        z_gather(i, 0)
    a_core_back()
    for i in (2, 3):
        z_gather(i, 0)
    w_cols()
    u_y1()
    for i in (0, 1):
        z_gather(i, 1)
    x_finish(2)
    xr[3].step(1)
    u_yg0()
    for i in (2, 3):
        z_gather(i, 1)
    a_done()
    inv_start()
    coarse(2)
    w_z()
    u_yg1()
    r_add(2)
    coarse(2)
    for i in (0, 1):
        z_gather(i, 2)
    x_finish(3)
    r_add(3)
    r_core()
    for i in (2, 3):
        z_gather(i, 2)
    w_x()
    u_core_back()
    coarse(4)
    store(m0, m0_out)
    for i in (0, 1):
        z_gather(i, 3)
    r_y0()
    for i in (2, 3):
        z_gather(i, 3)
    u_done()
    store(uf, uf_out)
    coarse(1)
    r_y1()
    fine()
    w_done()
    inv_end()
    for i in range(CHUNKS):
        zg[i].finish()
    store(vf, vf_out)
    for i in range(CHUNKS):
        update(i)
    for block in range(CHUNKS):
        where = jnp.int32(0)
        for chunk in range(1, CHUNKS):
            where = jnp.where(order[chunk] == block, chunk, where)
        out[:, block * PANEL : (block + 1) * PANEL] = mp[where]
    r_done()
    respond()
    for copy in stores:
        copy.wait()
    sends.drain()


def split(value):
    high = value.astype(BF16)
    return high, (value - high.astype(F32)).astype(BF16)


def dot(a, b, dims=(((1,), (0,)), ((), ()))):
    return lax.dot_general(a, b, dims, preferred_element_type=F32)


def dot3(a, b, dims=(((1,), (0,)), ((), ()))):
    return dot(a[0], b[0], dims) + (dot(a[0], b[1], dims) + dot(a[1], b[0], dims))


def invert(af, x_ref):
    n = 2 * PANEL
    a = af[...]
    eye = jnp.where(
        lax.broadcasted_iota(jnp.int32, (n, n), 0) == lax.broadcasted_iota(jnp.int32, (n, n), 1), 1.0, 0.0
    ).astype(F32)
    size = jnp.abs(a)
    scale = 1.0 / (jnp.max(jnp.sum(size, axis=0, keepdims=True)) * jnp.max(jnp.sum(size, axis=1, keepdims=True)))
    a_high, a_low = split(a)
    x_ref[...] = a.T * scale

    def coarse(state):
        count, _ = state
        x = x_ref[...]
        x_high = x.astype(BF16)
        rest = eye - dot(a_high, x_high)
        x_ref[...] = x + dot(x_high, rest.astype(BF16))
        return count + 1, jnp.sum(rest * rest)

    _, left = lax.while_loop(lambda s: (s[0] < 24) & (s[1] > 0.1), coarse, (jnp.int32(0), jnp.float32(1e9)))

    def fine(state):
        count, _ = state
        x = x_ref[...]
        x_parts = split(x)
        rest = eye - dot3((a_high, a_low), x_parts)
        x_ref[...] = x + dot3(x_parts, split(rest))
        return count + 1, jnp.sum(rest * rest)

    start = jnp.where(left < 0.5, 0, 100).astype(jnp.int32)
    count, left = lax.while_loop(lambda s: (s[0] < 6) & (s[1] > 1e-6), fine, (start, jnp.float32(1e9)))

    def exact(a, b):
        return jnp.dot(a, b, precision=lax.Precision.HIGHEST, preferred_element_type=F32)

    @pl.when(left > 1e-6)
    def _():
        x_ref[...] = af[...].T * scale

        def full(state):
            count, _ = state
            x = x_ref[...]
            rest = eye - exact(af[...], x)
            x_ref[...] = x + exact(x, rest)
            return count + 1, jnp.sum(rest * rest)

        lax.while_loop(lambda s: (s[0] < 60) & (s[1] > 1e-7), full, (jnp.int32(0), jnp.float32(1e9)))


def repair_kernel(
    sizes, residual, pivots, af_in, uf_in, vf_in, m0_in, r0_in, w_in, out_old, answer_old, out_new, answer_new,
    af, uf, vf, m0, r0, w, out, answer, x_ref, l_ref, mp, sem, sems,
):
    quarter = PANEL // CHUNKS
    parts = [pl.ds(i * quarter, quarter) for i in range(CHUNKS)]
    pairs = [(out_old.at[p], out.at[p], out_new.at[p]) for p in parts] + [(answer_old, answer, answer_new)]
    moves = [
        (pltpu.make_async_copy(a, b, sems.at[0, i]), pltpu.make_async_copy(b, c, sems.at[1, i]))
        for i, (a, b, c) in enumerate(pairs)
    ]
    for first, _ in moves:
        first.start()
    for first, second in moves:
        first.wait()
        second.start()
    for _, second in moves:
        second.wait()

    @pl.when(~(residual[0] < 1e-5))
    def _():
        for source, target in [(af_in, af), (uf_in, uf), (vf_in, vf), (m0_in, m0), (r0_in, r0), (w_in, w)]:
            copy = pltpu.make_async_copy(source, target, sem)
            copy.start()
            copy.wait()
        n_t, n_r, n_c = sizes
        t, z, col = lax.axis_index("term"), lax.axis_index("row"), lax.axis_index("col")
        group = z * n_t + t
        order, own_first, own_second = chunk_order(pivots, col)
        own_both = own_first & own_second
        invert(af, x_ref)
        inverse = split(x_ref[...])
        l_ref[...] = dot3(split(uf[...]), inverse)
        is_first, is_second = group == pivots[0], group == pivots[1]

        @pl.when(is_first)
        def _():
            l_ref[...] = -x_ref[:PANEL, :]

        @pl.when(is_second)
        def _():
            l_ref[...] = -x_ref[PANEL:, :]

        keep = jnp.where(is_first | is_second, 0.0, 1.0).astype(F32)
        left = split(l_ref[...])
        for chunk in range(CHUNKS):
            rows = vf[order[chunk]]
            value = m0[chunk] * keep - dot3(left, split(rows))
            if chunk == 0:
                value = jnp.where(
                    own_first, -l_ref[:, :PANEL], jnp.where(own_second, -l_ref[:, PANEL:], value)
                )
            if chunk == 1:
                value = jnp.where(own_both, -l_ref[:, PANEL:], value)
            mp[chunk] = value
        for block in range(CHUNKS):
            where = jnp.int32(0)
            for chunk in range(1, CHUNKS):
                where = jnp.where(order[chunk] == block, chunk, where)
            out[:, block * PANEL : (block + 1) * PANEL] = mp[where]
        both = dot3(left, split(w[...])).T
        rows = answer.shape[0]
        answer[...] = r0[...] - jnp.where(lax.rem(col, CORES) == 0, both[:rows], both[rows:])
        for source, target in [(out, out_new), (answer, answer_new)]:
            copy = pltpu.make_async_copy(source, target, sem)
            copy.start()
            copy.wait()


VMEM = pl.BlockSpec(memory_space=pltpu.VMEM)
SMEM = pl.BlockSpec(memory_space=pltpu.SMEM)
ANY = pl.BlockSpec(memory_space=pl.ANY)
LIMIT = 63 * 1024 * 1024
DMA = pltpu.SemaphoreType.DMA


def on_device(sizes, coupling, radial, energies, labels, pivot_blocks, probes):
    n_t, n_r, n_c = sizes
    n_y = n_c // CORES
    tile = coupling.shape[1]
    wide = 2 * PANEL
    z_rows = wide // n_r
    f32 = lambda *shape: pltpu.VMEM(shape, F32)
    width = probes.shape[1] // CORES
    shape = lambda *dims: jax.ShapeDtypeStruct(dims, F32)
    i32 = lambda *dims: pltpu.VMEM(dims, jnp.int32)
    bf16 = lambda *dims: pltpu.VMEM(dims, BF16)
    count = probes.shape[1]
    out, answer, residual, m0, vf, uf, af, r0, w = pl.pallas_call(
        functools.partial(exchange_kernel, sizes),
        out_shape=(
            shape(PANEL, tile),
            shape(count // n_c, PANEL),
            shape(1),
            shape(CHUNKS, PANEL, PANEL),
            shape(CHUNKS, wide, PANEL),
            shape(PANEL, wide),
            shape(wide, wide),
            shape(count // n_c, PANEL),
            shape(wide, count // n_y),
        ),
        in_specs=[ANY] * 6,
        out_specs=(VMEM, VMEM, SMEM) + (ANY,) * 4 + (VMEM,) * 2,
        scratch_shapes=[
            bf16(coupling.shape[0], CHUNKS, PANEL, tile),
            pltpu.SMEM(radial.shape, F32),
            f32(energies.shape[0] // 128, 128),
            i32(labels.shape[0] // 128, 128),
            pltpu.SMEM(pivot_blocks.shape, jnp.int32),
            f32(*probes.shape),
            bf16(CHUNKS, PANEL, count),
            bf16(CHUNKS, PANEL, count),
            f32(CHUNKS, PANEL, PANEL),
            f32(CHUNKS, wide, PANEL),
            f32(PANEL, wide),
            f32(wide, wide),
            f32(wide, wide),
            bf16(wide, wide),
            bf16(wide, wide),
            f32(PANEL, wide),
            f32(CHUNKS, PANEL, PANEL),
            f32(2, CHUNKS, PANEL, PANEL),
            f32(CHUNKS, CHUNKS, PANEL, PANEL),
            f32(CHUNKS, tile, PANEL),
            f32(tile // 128, 128, 128),
            f32(CHUNKS, 2, n_t // 2, PANEL, PANEL),
            f32(CHUNKS, 2, n_r // 2, z_rows, PANEL),
            f32(CHUNKS, 2, z_rows // 2, PANEL),
            f32(CHUNKS, z_rows, PANEL),
            f32(CHUNKS, n_t - 1, z_rows // n_t, PANEL),
            f32(wide, wide),
            f32(PANEL, wide),
            f32(PANEL, wide),
            f32(2, n_y // 2, PANEL // n_y, wide),
            f32(PANEL // n_y, wide),
            f32(n_r - 1, PANEL // n_y // n_r, wide),
            f32(PANEL // n_y // n_r, wide),
            f32(n_t, PANEL // n_y // n_r, wide),
            f32(PANEL, wide),
            f32(PANEL // CORES, wide),
            f32(PANEL // CORES, wide),
            f32(2, n_y // 2, PANEL // CORES // n_y, wide),
            f32(PANEL, count),
            f32(CORES, width, PANEL),
            f32(width, PANEL),
            f32(width, PANEL),
            f32(2, n_y // 2, width // n_y, PANEL),
            f32(n_y, z_rows // n_t, count // n_y),
            f32(n_c - 1, z_rows // n_t, count // n_y),
            f32(n_t, n_r * (z_rows // n_t), count // n_y),
            DMA((5 + CHUNKS,)), DMA((3 + CHUNKS,)),
            DMA((CHUNKS, 2, 3)), DMA((CHUNKS, 2, 3)),
            DMA((CHUNKS, 2, n_r // 2)), DMA((CHUNKS, 2, n_r // 2)),
            DMA((CHUNKS, n_t - 1)), DMA((CHUNKS, n_t - 1)),
            DMA((CHUNKS, n_t - 1)), DMA((CHUNKS, n_t - 1)),
            DMA((CHUNKS, 2, n_r // 2)), DMA((CHUNKS, 2, n_r // 2)),
            DMA((5,)), DMA((5,)),
            DMA((2, 3)), DMA((2, 3)),
            DMA((n_r - 1,)), DMA((n_r - 1,)),
            DMA((n_t - 1,)), DMA((n_t - 1,)),
            DMA((n_r - 1,)), DMA((n_r - 1,)),
            DMA((2, 2)), DMA((2, 2)),
            DMA((2, 3)), DMA((2, 3)),
            DMA((2, 2)), DMA((2, 2)),
            DMA((2, 3)), DMA((2, 3)),
            DMA((n_c - 1,)), DMA((n_c - 1,)),
            DMA((n_r - 1,)), DMA((n_r - 1,)),
            DMA((n_t - 1,)), DMA((n_t - 1,)),
        ],
        compiler_params=pltpu.CompilerParams(
            collective_id=0, has_side_effects=True, vmem_limit_bytes=LIMIT
        ),
        name="exchange",
    )(coupling, radial, energies.reshape(-1, 128), labels.reshape(-1, 128), pivot_blocks, probes)
    return pl.pallas_call(
        functools.partial(repair_kernel, sizes),
        out_shape=(shape(PANEL, tile), shape(count // n_c, PANEL)),
        in_specs=[SMEM, SMEM] + [ANY] * 8,
        out_specs=(ANY, ANY),
        scratch_shapes=[
            f32(wide, wide), f32(PANEL, wide), f32(CHUNKS, wide, PANEL), f32(CHUNKS, PANEL, PANEL),
            f32(count // n_c, PANEL), f32(wide, count // n_y), f32(PANEL, tile), f32(count // n_c, PANEL),
            f32(wide, wide), f32(PANEL, wide), f32(CHUNKS, PANEL, PANEL), DMA, DMA((2, CHUNKS + 1)),
        ],
        compiler_params=pltpu.CompilerParams(vmem_limit_bytes=LIMIT),
        name="repair",
    )(residual, pivot_blocks, af, uf, vf, m0, r0, w, out, answer)


def solution(mesh):
    sizes = tuple(mesh.shape[name] for name in ("term", "row", "col"))
    return jax.shard_map(
        functools.partial(on_device, sizes),
        mesh=mesh,
        in_specs=(P("term", "row", "col"), P(), P(), P(), P(), P("col", None)),
        out_specs=(P(("row", "term"), "col"), P("col", ("row", "term"))),
        check_vma=False,
    )
```

```python
import functools

import jax
import jax.numpy as jnp
from jax import lax
from jax.experimental import pallas as pl
from jax.experimental.pallas import tpu as pltpu
from jax.sharding import PartitionSpec as P

MESH = pl.DeviceIdType.MESH
PANEL = 256
CHUNKS = 4
CORES = 2
F32 = jnp.float32
BF16 = jnp.bfloat16
STEP = 0.25


def aligned(index, step):
    return pl.multiple_of(index, step)


class Sends:
    def __init__(self):
        self.copies = []

    def start(self, source, target, send_sem, recv_sem, device):
        copy = pltpu.make_async_remote_copy(
            src_ref=source,
            dst_ref=target,
            send_sem=send_sem,
            recv_sem=recv_sem,
            device_id=device,
            device_id_type=MESH,
        )
        copy.start()
        self.copies.append(copy)
        return copy

    def drain(self):
        for copy in self.copies:
            copy.wait_send()
        self.copies = []


class RingReduce:
    def __init__(self, sends, device_at, pos, n, rows, own, slots, send_sem, recv_sem, source=None, stage=None):
        self.sends, self.device_at, self.pos, self.n, self.rows = sends, device_at, pos, n, rows
        self.own, self.slots, self.send_sem, self.recv_sem = own, slots, send_sem, recv_sem
        self.source, self.stage = source, stage
        self.half = rows // 2
        self.reach = n // 2
        self.sent = {}

    def neighbour(self, way):
        return self.device_at(lax.rem(self.pos + (1 if way == 0 else self.n - 1), self.n))

    def dest(self, way, distance):
        return lax.rem(self.pos + (distance if way == 0 else self.n - distance), self.n)

    def send(self, way, key, source, target):
        self.sent[way, key] = self.sends.start(
            source, target, self.send_sem.at[way, key], self.recv_sem.at[way, key], self.neighbour(way)
        )

    def start(self):
        half = self.half
        for way in range(2):
            dest = self.dest(way, self.reach)
            low = way * half
            if self.source is not None:
                source = self.source.at[pl.ds(aligned(dest * self.rows + low, half), half)]
            else:
                self.stage[way] = self.own(dest, low, half)
                source = self.stage.at[way]
            self.send(way, 0, source, self.slots.at[way, 0, pl.ds(low, half)])
        if self.source is not None:
            for way in range(2):
                dest = self.dest(way, self.reach - 1)
                other = (1 - way) * half
                source = self.source.at[pl.ds(aligned(dest * self.rows + other, half), half)]
                self.send(way, self.reach, source, self.slots.at[way, 1, pl.ds(other, half)])

    def step(self, s):
        half = self.half
        for way in range(2):
            self.sent[way, s - 1].wait_recv()
            dest = self.dest(way, self.reach - s)
            low, other = way * half, (1 - way) * half
            if s == 1:
                self.slots[way, 0, low : low + half] += self.own(dest, low, half)
                if self.source is not None:
                    part = pl.ds(low, half)
                    self.send(way, 1, self.slots.at[way, 0, part], self.slots.at[way, 1, part])
                    continue
                self.slots[way, 0, other : other + half] = self.own(dest, other, half)
            else:
                self.slots[way, s - 1] += self.own(dest, 0, self.rows)
            self.send(way, s, self.slots.at[way, s - 1], self.slots.at[way, s])

    def finish(self):
        for way in range(2):
            self.sent[way, self.reach - 1].wait_recv()
            if self.source is not None:
                self.sent[way, self.reach].wait_recv()
        last = self.reach - 1
        return self.own(self.pos, 0, self.rows) + (self.slots[0, last] + self.slots[1, last])


class RingGather:
    def __init__(self, sends, device_at, pos, n, rows, ref, base, send_sem, recv_sem):
        self.sends, self.device_at, self.pos, self.n, self.rows = sends, device_at, pos, n, rows
        self.ref, self.base, self.send_sem, self.recv_sem = ref, base, send_sem, recv_sem
        self.reach = n // 2
        self.sent = {}

    def step(self, s):
        n = self.n
        for way in range(2):
            if s > 0:
                self.sent[way, s - 1].wait_recv()
            block = lax.rem(self.pos + (n - s if way == 0 else s), n)
            to = self.device_at(lax.rem(self.pos + (1 if way == 0 else n - 1), n))
            rows = self.rows if s < self.reach - 1 else self.rows // 2
            low = 0 if s < self.reach - 1 else way * rows
            part = self.ref.at[pl.ds(aligned(self.base + block * self.rows + low, rows), rows)]
            self.sent[way, s] = self.sends.start(part, part, self.send_sem.at[way, s], self.recv_sem.at[way, s], to)

    def finish(self):
        for way in range(2):
            self.sent[way, self.reach - 1].wait_recv()


def chunk_order(pivots, col):
    first, second = pivots[0], pivots[1]
    own_first = first // CHUNKS == col
    own_second = second // CHUNKS == col
    local_first, local_second = lax.rem(first, CHUNKS), lax.rem(second, CHUNKS)
    lead = jnp.where(own_first, local_first, jnp.where(own_second, local_second, 0))
    order = [lead] + [jnp.where(lead == i, 0, i) for i in range(1, CHUNKS)]
    both = own_first & own_second
    next_up = order[1]
    for i in range(2, CHUNKS):
        order[i] = jnp.where(both & (order[i] == local_second), next_up, order[i])
    order[1] = jnp.where(both, local_second, order[1])
    return order, own_first, own_second


def exchange_kernel(
    sizes, coupling_in, radial_in, energies_in, labels_in, pivots_in, probes_in,
    out, answer, left_out, m0_out, vf_out, uf_out, af_out, r0, w,
    coupling, radial, energies, labels, pivots, probes, p_high, p_low, m0, vf, uf, af, x_ref, a_high, a_low, l_ref,
    vsrc, qn, q, parity, x_slots, z_slots, z_stage, z_mine, z_parts, am, ac, ah, a_slots, a_mine, az, ax_mine, ax,
    um, uc, uh, u_slots, reply, part, r_half, r_got, r_slots, w_mine, w_slots, w_all,
    in_s, out_s,
    x_ss, x_rs, z_ss, z_rs, zx_ss, zx_rs, zg_ss, zg_rs, zy_ss, zy_rs,
    c_ss, c_rs, ay_ss, ay_rs, az_ss, az_rs, ax_ss, ax_rs, ag_ss, ag_rs, ayg_ss, ayg_rs,
    uy_ss, uy_rs, uyg_ss, uyg_rs, ry_ss, ry_rs, wc_ss, wc_rs, wz_ss, wz_rs, wx_ss, wx_rs,
):
    n_t, n_r, n_c = sizes
    n_y = n_c // CORES
    t, z, col = lax.axis_index("term"), lax.axis_index("row"), lax.axis_index("col")
    y, core = col // CORES, lax.rem(col, CORES)
    sends = Sends()
    loads = [
        pltpu.make_async_copy(source, target, in_s.at[i])
        for i, (source, target) in enumerate(
            [(pivots_in, pivots), (radial_in, radial), (labels_in, labels), (energies_in, energies)]
        )
    ]
    blocks = [
        pltpu.make_async_copy(
            coupling_in.at[:, pl.ds(i * PANEL, PANEL)], coupling.at[:, i], in_s.at[4 + i]
        )
        for i in range(CHUNKS)
    ]
    trials = pltpu.make_async_copy(probes_in, probes, in_s.at[4 + CHUNKS])
    for copy in loads + blocks:
        copy.start()

    def at_x(p):
        return {"term": p}

    def at_z(p):
        return {"row": p}

    def at_y(p):
        return {"col": p * CORES + core}

    other_core = {"col": y * CORES + (1 - core)}
    greet = [at_x(lax.rem(t + d, n_t)) for d in range(1, n_t)]
    greet += [at_z(lax.rem(z + d, n_r)) for d in range(1, n_r)]
    greet += [{"col": lax.rem(col + d, n_c)} for d in range(1, n_c)]
    barrier = pltpu.get_barrier_semaphore()
    for device in greet:
        pl.semaphore_signal(barrier, inc=1, device_id=device, device_id_type=MESH)

    for copy in loads:
        copy.wait()
    order, own_first, own_second = chunk_order(pivots, col)
    own_both = own_first & own_second
    piv = (pivots[0], pivots[1])
    col_owned = (own_first, own_second)
    col_chunk = (jnp.int32(0), jnp.where(own_first, 1, 0))

    lab = labels[pl.ds(aligned(z * 8, 8), 8), :]
    lab = lax.rem(lab, 2).astype(F32)
    for b in range(8):
        parity[b] = jnp.broadcast_to(lab[b : b + 1, :], (128, 128)).T

    even = radial[2 * t] * STEP
    odd = radial[2 * t + 1] * STEP
    on_diagonal = jnp.where((z == col) & (t == 0), 1.0, 0.0).astype(F32)

    def column_rows(table, block):
        return [table[pl.ds(col * 8 + block * 2 + i, 1), :] for i in range(2)]

    def layers(group, half, rows, block, col_par, i):
        cols = slice(block * PANEL + i * 128, block * PANEL + (i + 1) * 128)
        c0 = coupling[0, group, rows, cols].astype(F32) * even
        c1 = coupling[1, group, rows, cols].astype(F32) * odd
        return jnp.where(parity[group * 2 + half] == col_par[i], c0, c1)

    same = lax.broadcasted_iota(jnp.int32, (128, 128), 0) == lax.broadcasted_iota(jnp.int32, (128, 128), 1)

    def fill_pivot(k):
        group = lax.rem(piv[k], CHUNKS)
        mine = piv[k] // CHUNKS == z
        for block in range(CHUNKS):
            col_par = [lax.rem(v, 2).astype(F32) for v in column_rows(labels, block)]
            diag = [(1.0 + STEP * v) * on_diagonal for v in column_rows(energies, block)]
            for half in range(2):
                rows = slice(half * 128, (half + 1) * 128)
                for i in range(2):
                    value = layers(group, half, rows, block, col_par, i)
                    if i == half:
                        value = value + jnp.where(same & (group == block), diag[i], 0.0)
                    vsrc[k, block, rows, i * 128 : (i + 1) * 128] = jnp.where(mine, value, 0.0)

    def fill(block):
        col_par = [lax.rem(v, 2).astype(F32) for v in column_rows(labels, block)]

        def body(group, carry):
            for half in range(2):
                rows = slice(half * 128, (half + 1) * 128)
                for i in range(2):
                    qn[block, group, rows, i * 128 : (i + 1) * 128] = layers(group, half, rows, block, col_par, i)
            return carry

        lax.fori_loop(0, CHUNKS, body, 0)
        for i, v in enumerate(column_rows(energies, block)):
            part = slice(i * 128, (i + 1) * 128)
            qn[block, block, part, part] += jnp.where(same, (1.0 + STEP * v) * on_diagonal, 0.0)

    def take(chunk):
        for i in range(CHUNKS):
            q[chunk, i * PANEL : (i + 1) * PANEL, :] = qn[order[chunk], i]

    def x_own(chunk):
        return lambda dest, low, n: q[chunk, pl.ds(aligned(dest * PANEL + low, 128), n), :]

    xr = [
        RingReduce(
            sends, at_x, t, n_t, PANEL, x_own(i), x_slots.at[i], x_ss.at[i], x_rs.at[i], source=q.at[i]
        )
        for i in range(CHUNKS)
    ]

    def x_finish(i):
        m0[i] = xr[i].finish()

    z_rows = 2 * PANEL // n_r

    def z_own(h):
        def load(dest, low, n):
            per = PANEL // z_rows
            which = jnp.where(dest < per, 0, 1)
            return vsrc[which, h, pl.ds(aligned(lax.rem(dest, per) * z_rows + low, 32), n), :]

        return load

    zr = [
        RingReduce(
            sends, at_z, z, n_r, z_rows, z_own(h), z_slots.at[h], z_ss.at[h], z_rs.at[h], stage=z_stage.at[h]
        )
        for h in range(CHUNKS)
    ]
    zg = [
        RingGather(sends, at_z, z, n_r, z_rows, vf.at[h], 0, zy_ss.at[h], zy_rs.at[h]) for h in range(CHUNKS)
    ]
    piece = z_rows // n_t
    zx = [{} for _ in range(CHUNKS)]
    zxg = [{} for _ in range(CHUNKS)]

    def z_finish(h):
        z_mine[h] = zr[h].finish()
        for d in range(1, n_t):
            dest = lax.rem(t + d, n_t)
            zx[h][d] = sends.start(
                z_mine.at[h, pl.ds(aligned(dest * piece, piece), piece)],
                z_parts.at[h, d - 1],
                zx_ss.at[h, d - 1],
                zx_rs.at[h, d - 1],
                at_x(dest),
            )

    def z_sum(h):
        for d in range(1, n_t):
            zx[h][d].wait_recv()
        total = z_mine[h, pl.ds(aligned(t * piece, piece), piece), :]
        for d in range(1, n_t):
            total = total + z_parts[h, d - 1]
        mine = pl.ds(aligned(z * z_rows + t * piece, piece), piece)
        vf[h, mine, :] = total
        for d in range(1, n_t):
            dest = lax.rem(t + d, n_t)
            zxg[h][d] = sends.start(
                vf.at[h, mine], vf.at[h, mine], zg_ss.at[h, d - 1], zg_rs.at[h, d - 1], at_x(dest)
            )

    def z_gather(h, s):
        if s == 0:
            for d in range(1, n_t):
                zxg[h][d].wait_recv()
        zg[h].step(s)

    def a_load():
        for k in range(2):
            for l in range(2):
                am[k * PANEL : (k + 1) * PANEL, l * PANEL : (l + 1) * PANEL] = jnp.where(
                    col_owned[l], vsrc[k, lax.rem(piv[l], CHUNKS)], 0.0
                )

    a_ring = RingReduce(
        sends, at_y, y, n_y, PANEL // n_y,
        lambda dest, low, n: ah[pl.ds(aligned(dest * (PANEL // n_y) + low, 32), n), :],
        a_slots, ay_ss, ay_rs, source=ah,
    )
    a_state = {}

    def a_core():
        a_load()
        a_state["core"] = sends.start(
            am.at[pl.ds(aligned((1 - core) * PANEL, PANEL), PANEL)], ac, c_ss.at[0], c_rs.at[0], other_core
        )

    def a_y0():
        a_state["core"].wait_recv()
        ah[...] = am[pl.ds(aligned(core * PANEL, PANEL), PANEL), :] + ac[...]
        a_ring.start()

    def a_y1():
        a_ring.step(1)

    a_rows = PANEL // n_y
    a_piece = a_rows // n_r

    def a_z():
        a_mine[...] = a_ring.finish()
        a_state["z"] = []
        for d in range(1, n_r):
            dest = lax.rem(z + d, n_r)
            a_state["z"].append(
                sends.start(
                    a_mine.at[pl.ds(aligned(dest * a_piece, a_piece), a_piece)],
                    az.at[d - 1],
                    az_ss.at[d - 1],
                    az_rs.at[d - 1],
                    at_z(dest),
                )
            )

    def a_x():
        for copy in a_state["z"]:
            copy.wait_recv()
        total = a_mine[pl.ds(aligned(z * a_piece, a_piece), a_piece), :]
        for d in range(1, n_r):
            total = total + az[d - 1]
        ax_mine[...] = total
        ax[t] = total
        a_state["x"] = []
        for d in range(1, n_t):
            a_state["x"].append(
                sends.start(ax_mine, ax.at[t], ax_ss.at[d - 1], ax_rs.at[d - 1], at_x(lax.rem(t + d, n_t)))
            )

    def a_back():
        for copy in a_state["x"]:
            copy.wait_recv()
        total = ax[0]
        for d in range(1, n_t):
            total = total + ax[d]
        mine = pl.ds(aligned(core * PANEL + y * a_rows + z * a_piece, a_piece), a_piece)
        af[mine, :] = total
        a_state["zg"] = [
            sends.start(
                af.at[mine], af.at[mine], ag_ss.at[d - 1], ag_rs.at[d - 1], at_z(lax.rem(z + d, n_r))
            )
            for d in range(1, n_r)
        ]

    a_gather = RingGather(sends, at_y, y, n_y, a_rows, af, core * PANEL, ayg_ss, ayg_rs)

    def a_yg0():
        for copy in a_state["zg"]:
            copy.wait_recv()
        a_gather.step(0)

    def a_yg1():
        a_gather.step(1)

    def a_core_back():
        a_gather.finish()
        part = af.at[pl.ds(aligned(core * PANEL, PANEL), PANEL)]
        a_state["core"] = sends.start(part, part, c_ss.at[1], c_rs.at[1], other_core)

    def a_done():
        a_state["core"].wait_recv()

    u_half = PANEL // CORES
    u_rows = u_half // n_y
    u_ring = RingReduce(
        sends, at_y, y, n_y, u_rows,
        lambda dest, low, n: uh[pl.ds(aligned(dest * u_rows + low, 16), n), :],
        u_slots, uy_ss, uy_rs, source=uh,
    )
    u_gather = RingGather(sends, at_y, y, n_y, u_rows, uf, core * u_half, uyg_ss, uyg_rs)
    u_state = {}

    def u_core():
        for l in range(2):
            um[:, l * PANEL : (l + 1) * PANEL] = jnp.where(col_owned[l], m0[col_chunk[l]], 0.0)
        u_state["core"] = sends.start(
            um.at[pl.ds(aligned((1 - core) * u_half, u_half), u_half)], uc, c_ss.at[2], c_rs.at[2], other_core
        )

    def u_y0():
        u_state["core"].wait_recv()
        uh[...] = um[pl.ds(aligned(core * u_half, u_half), u_half), :] + uc[...]
        u_ring.start()

    def u_y1():
        u_ring.step(1)

    def u_yg0():
        uf[pl.ds(aligned(core * u_half + y * u_rows, u_rows), u_rows), :] = u_ring.finish()
        u_gather.step(0)

    def u_yg1():
        u_gather.step(1)

    def u_core_back():
        u_gather.finish()
        part = uf.at[pl.ds(aligned(core * u_half, u_half), u_half)]
        u_state["core"] = sends.start(part, part, c_ss.at[3], c_rs.at[3], other_core)

    def u_done():
        u_state["core"].wait_recv()

    n = 2 * PANEL
    eye = lambda: jnp.where(
        lax.broadcasted_iota(jnp.int32, (n, n), 0) == lax.broadcasted_iota(jnp.int32, (n, n), 1), 1.0, 0.0
    ).astype(F32)
    stores = []

    def store(source, target):
        copy = pltpu.make_async_copy(source, target, out_s.at[len(stores)])
        copy.start()
        stores.append(copy)

    def split_trials():
        trials.wait()
        for i in range(CHUNKS):
            p_high[i], p_low[i] = split(probes[i * PANEL : (i + 1) * PANEL, :])

    def inv_start():
        store(af, af_out)
        high, low = split(af[...])
        a_high[...], a_low[...] = high, low
        square = dot(high, high, (((0,), (0,)), ((), ())))
        x_ref[...] = af[...].T * (1.8 / jnp.max(jnp.sum(jnp.abs(square), axis=0, keepdims=True)))

    def coarse(count):
        def body(i, carry):
            x = x_ref[...]
            high = x.astype(BF16)
            rest = eye() - dot(a_high[...], high)
            x_ref[...] = x + dot(high, rest.astype(BF16))
            return carry

        lax.fori_loop(0, count, body, 0)

    def fine():
        x = x_ref[...]
        x_parts = split(x)
        rest = eye() - dot3((a_high[...], a_low[...]), x_parts)
        x_ref[...] = x + dot(x_parts[0], rest.astype(BF16))
        return jnp.sum(rest * rest)

    group = z * n_t + t
    is_first, is_second = group == piv[0], group == piv[1]
    keep = jnp.where(is_first | is_second, 0.0, 1.0).astype(F32)
    state = {}

    def inv_end():
        left_out[0] = fine()
        x = x_ref[...]
        factor = dot3(split(uf[...]), split(x))
        factor = jnp.where(is_first, -x[:PANEL, :], jnp.where(is_second, -x[PANEL:, :], factor))
        l_ref[...] = factor
        state["left"] = split(factor)

    def update(block):
        where = jnp.int32(0)
        for chunk in range(1, CHUNKS):
            where = jnp.where(order[chunk] == block, chunk, where)
        value = m0[where] * keep - dot3(state["left"], split(vf[block]))
        for l in range(2):
            here = col_owned[l] & (lax.rem(piv[l], CHUNKS) == block)
            value = jnp.where(here, -l_ref[:, l * PANEL : (l + 1) * PANEL], value)
        out[:, block * PANEL : (block + 1) * PANEL] = value

    def r_add(chunk):
        factor = keep
        if chunk == 0:
            factor = jnp.where(own_first | own_second, 0.0, keep)
        if chunk == 1:
            factor = jnp.where(own_both, 0.0, keep)
        add = dot3(split(m0[chunk] * factor), (p_high[order[chunk]], p_low[order[chunk]]))
        if chunk == 0:
            reply[...] = add
        else:
            reply[...] += add

    r_rows = part.shape[1] // n_y
    r_ring = RingReduce(
        sends, at_y, y, n_y, r_rows,
        lambda dest, low, n: r_half[pl.ds(aligned(dest * r_rows + low, 32), n), :],
        r_slots, ry_ss, ry_rs, source=r_half,
    )

    def r_core():
        turned = reply[...].T
        for j in range(n_c):
            part[j % CORES, (j // CORES) * r_rows : (j // CORES + 1) * r_rows, :] = turned[
                j * r_rows : (j + 1) * r_rows, :
            ]
        state["r"] = sends.start(part.at[1 - core], r_got, c_ss.at[4], c_rs.at[4], other_core)

    def r_y0():
        state["r"].wait_recv()
        r_half[...] = part[core] + r_got[...]
        r_ring.start()

    def r_y1():
        r_ring.step(1)

    def r_done():
        r0[...] = r_ring.finish()

    lanes = w_mine.shape[2]

    def w_cols():
        first = z * z_rows + t * piece
        row_id = lax.broadcasted_iota(jnp.int32, (piece, PANEL), 0) + first
        col_id = lax.broadcasted_iota(jnp.int32, (piece, PANEL), 1)
        total = jnp.zeros((piece, probes.shape[1]), F32)
        for h in range(CHUNKS):
            value = vf[h, pl.ds(aligned(first, piece), piece), :]
            for l in range(2):
                here = col_owned[l] & (lax.rem(piv[l], CHUNKS) == h)
                unit = jnp.where(row_id == col_id + l * PANEL, 1.0, 0.0).astype(F32)
                value = jnp.where(here, unit, value)
            total = total + dot3(split(value), (p_high[h], p_low[h]))
        for i in range(n_y):
            w_mine[i] = total[:, i * lanes : (i + 1) * lanes]
        state["wc"] = []
        for d in range(1, n_c):
            dest = lax.rem(col + d, n_c)
            state["wc"].append(
                sends.start(
                    w_mine.at[dest // CORES], w_slots.at[d - 1], wc_ss.at[d - 1], wc_rs.at[d - 1], {"col": dest}
                )
            )

    def w_z():
        total = w_mine[y]
        for d in range(1, n_c):
            state["wc"][d - 1].wait_recv()
            total = total + w_slots[d - 1]
        mine = pl.ds(aligned(z * piece, piece), piece)
        w_all[t, mine, :] = total
        state["wz"] = [
            sends.start(
                w_all.at[t, mine], w_all.at[t, mine], wz_ss.at[d - 1], wz_rs.at[d - 1], at_z(lax.rem(z + d, n_r))
            )
            for d in range(1, n_r)
        ]

    def w_x():
        for copy in state["wz"]:
            copy.wait_recv()
        state["wx"] = [
            sends.start(w_all.at[t], w_all.at[t], wx_ss.at[d - 1], wx_rs.at[d - 1], at_x(lax.rem(t + d, n_t)))
            for d in range(1, n_t)
        ]

    def w_done():
        for copy in state["wx"]:
            copy.wait_recv()
        for i in range(n_t):
            for j in range(n_r):
                first = j * z_rows + i * piece
                w[first : first + piece, :] = w_all[i, j * piece : (j + 1) * piece, :]

    def respond():
        both = dot3(state["left"], split(w[...])).T
        answer[...] = r0[...] - jnp.where(core == 0, both[:r_rows], both[r_rows:])

    for copy in blocks:
        copy.wait()
    fill_pivot(0)
    fill_pivot(1)
    pl.semaphore_wait(barrier, len(greet))
    for i in range(CHUNKS):
        zr[i].start()
    a_core()
    trials.start()
    fill(0)
    fill(1)
    for i in range(CHUNKS):
        zr[i].step(1)
    fill(2)
    fill(3)
    take(0)
    xr[0].start()
    a_y0()
    take(1)
    take(2)
    take(3)
    for i in (0, 1):
        zr[i].step(2)
    xr[0].step(1)
    xr[1].start()
    a_y1()
    for i in (2, 3):
        zr[i].step(2)
    split_trials()
    a_z()
    for i in (0, 1):
        zr[i].step(3)
    x_finish(0)
    a_x()
    for i in (2, 3):
        zr[i].step(3)
    xr[1].step(1)
    xr[2].start()
    a_back()
    for i in (0, 1):
        z_finish(i)
    a_yg0()
    for i in (2, 3):
        z_finish(i)
    x_finish(1)
    u_core()
    r_add(0)
    r_add(1)
    for i in (0, 1):
        z_sum(i)
    a_yg1()
    for i in (2, 3):
        z_sum(i)
    xr[2].step(1)
    xr[3].start()
    u_y0()
    for i in (0, 1):
        z_gather(i, 0)
    a_core_back()
    for i in (2, 3):
        z_gather(i, 0)
    w_cols()
    u_y1()
    for i in (0, 1):
        z_gather(i, 1)
    x_finish(2)
    xr[3].step(1)
    u_yg0()
    for i in (2, 3):
        z_gather(i, 1)
    a_done()
    inv_start()
    coarse(2)
    w_z()
    u_yg1()
    r_add(2)
    coarse(2)
    for i in (0, 1):
        z_gather(i, 2)
    x_finish(3)
    r_add(3)
    r_core()
    for i in (2, 3):
        z_gather(i, 2)
    w_x()
    u_core_back()
    coarse(4)
    store(m0, m0_out)
    for i in (0, 1):
        z_gather(i, 3)
    r_y0()
    for i in (2, 3):
        z_gather(i, 3)
    u_done()
    store(uf, uf_out)
    r_y1()
    fine()
    w_done()
    inv_end()
    zg[0].finish()
    store(vf.at[0], vf_out.at[0])
    update(0)
    zg[1].finish()
    store(vf.at[1], vf_out.at[1])
    update(1)
    zg[2].finish()
    store(vf.at[2], vf_out.at[2])
    update(2)
    zg[3].finish()
    store(vf.at[3], vf_out.at[3])
    update(3)
    r_done()
    respond()
    for copy in stores:
        copy.wait()
    sends.drain()


def split(value):
    high = value.astype(BF16)
    return high, (value - high.astype(F32)).astype(BF16)


def dot(a, b, dims=(((1,), (0,)), ((), ()))):
    return lax.dot_general(a, b, dims, preferred_element_type=F32)


def dot3(a, b, dims=(((1,), (0,)), ((), ()))):
    return dot(a[0], b[0], dims) + (dot(a[0], b[1], dims) + dot(a[1], b[0], dims))


def invert(af, x_ref):
    n = 2 * PANEL
    a = af[...]
    eye = jnp.where(
        lax.broadcasted_iota(jnp.int32, (n, n), 0) == lax.broadcasted_iota(jnp.int32, (n, n), 1), 1.0, 0.0
    ).astype(F32)
    size = jnp.abs(a)
    scale = 1.0 / (jnp.max(jnp.sum(size, axis=0, keepdims=True)) * jnp.max(jnp.sum(size, axis=1, keepdims=True)))
    a_high, a_low = split(a)
    x_ref[...] = a.T * scale

    def coarse(state):
        count, _ = state
        x = x_ref[...]
        x_high = x.astype(BF16)
        rest = eye - dot(a_high, x_high)
        x_ref[...] = x + dot(x_high, rest.astype(BF16))
        return count + 1, jnp.sum(rest * rest)

    _, left = lax.while_loop(lambda s: (s[0] < 24) & (s[1] > 0.1), coarse, (jnp.int32(0), jnp.float32(1e9)))

    def fine(state):
        count, _ = state
        x = x_ref[...]
        x_parts = split(x)
        rest = eye - dot3((a_high, a_low), x_parts)
        x_ref[...] = x + dot3(x_parts, split(rest))
        return count + 1, jnp.sum(rest * rest)

    start = jnp.where(left < 0.5, 0, 100).astype(jnp.int32)
    count, left = lax.while_loop(lambda s: (s[0] < 6) & (s[1] > 1e-6), fine, (start, jnp.float32(1e9)))

    def exact(a, b):
        return jnp.dot(a, b, precision=lax.Precision.HIGHEST, preferred_element_type=F32)

    @pl.when(left > 1e-6)
    def _():
        x_ref[...] = af[...].T * scale

        def full(state):
            count, _ = state
            x = x_ref[...]
            rest = eye - exact(af[...], x)
            x_ref[...] = x + exact(x, rest)
            return count + 1, jnp.sum(rest * rest)

        lax.while_loop(lambda s: (s[0] < 60) & (s[1] > 1e-7), full, (jnp.int32(0), jnp.float32(1e9)))


def repair_kernel(
    sizes, residual, pivots, af_in, uf_in, vf_in, m0_in, r0_in, w_in, out_old, answer_old, out_new, answer_new,
    af, uf, vf, m0, r0, w, out, answer, x_ref, l_ref, mp, sem, sems,
):
    quarter = PANEL // CHUNKS
    parts = [pl.ds(i * quarter, quarter) for i in range(CHUNKS)]
    pairs = [(out_old.at[p], out.at[p], out_new.at[p]) for p in parts] + [(answer_old, answer, answer_new)]
    moves = [
        (pltpu.make_async_copy(a, b, sems.at[0, i]), pltpu.make_async_copy(b, c, sems.at[1, i]))
        for i, (a, b, c) in enumerate(pairs)
    ]
    for first, _ in moves:
        first.start()
    for first, second in moves:
        first.wait()
        second.start()
    for _, second in moves:
        second.wait()

    @pl.when(~(residual[0] < 1e-5))
    def _():
        for source, target in [(af_in, af), (uf_in, uf), (vf_in, vf), (m0_in, m0), (r0_in, r0), (w_in, w)]:
            copy = pltpu.make_async_copy(source, target, sem)
            copy.start()
            copy.wait()
        n_t, n_r, n_c = sizes
        t, z, col = lax.axis_index("term"), lax.axis_index("row"), lax.axis_index("col")
        group = z * n_t + t
        order, own_first, own_second = chunk_order(pivots, col)
        own_both = own_first & own_second
        invert(af, x_ref)
        inverse = split(x_ref[...])
        l_ref[...] = dot3(split(uf[...]), inverse)
        is_first, is_second = group == pivots[0], group == pivots[1]

        @pl.when(is_first)
        def _():
            l_ref[...] = -x_ref[:PANEL, :]

        @pl.when(is_second)
        def _():
            l_ref[...] = -x_ref[PANEL:, :]

        keep = jnp.where(is_first | is_second, 0.0, 1.0).astype(F32)
        left = split(l_ref[...])
        for chunk in range(CHUNKS):
            rows = vf[order[chunk]]
            value = m0[chunk] * keep - dot3(left, split(rows))
            if chunk == 0:
                value = jnp.where(
                    own_first, -l_ref[:, :PANEL], jnp.where(own_second, -l_ref[:, PANEL:], value)
                )
            if chunk == 1:
                value = jnp.where(own_both, -l_ref[:, PANEL:], value)
            mp[chunk] = value
        for block in range(CHUNKS):
            where = jnp.int32(0)
            for chunk in range(1, CHUNKS):
                where = jnp.where(order[chunk] == block, chunk, where)
            out[:, block * PANEL : (block + 1) * PANEL] = mp[where]
        both = dot3(left, split(w[...])).T
        rows = answer.shape[0]
        answer[...] = r0[...] - jnp.where(lax.rem(col, CORES) == 0, both[:rows], both[rows:])
        for source, target in [(out, out_new), (answer, answer_new)]:
            copy = pltpu.make_async_copy(source, target, sem)
            copy.start()
            copy.wait()


VMEM = pl.BlockSpec(memory_space=pltpu.VMEM)
SMEM = pl.BlockSpec(memory_space=pltpu.SMEM)
ANY = pl.BlockSpec(memory_space=pl.ANY)
LIMIT = 63 * 1024 * 1024
DMA = pltpu.SemaphoreType.DMA


def on_device(sizes, coupling, radial, energies, labels, pivot_blocks, probes):
    n_t, n_r, n_c = sizes
    n_y = n_c // CORES
    tile = coupling.shape[1]
    wide = 2 * PANEL
    z_rows = wide // n_r
    f32 = lambda *shape: pltpu.VMEM(shape, F32)
    width = probes.shape[1] // CORES
    shape = lambda *dims: jax.ShapeDtypeStruct(dims, F32)
    i32 = lambda *dims: pltpu.VMEM(dims, jnp.int32)
    bf16 = lambda *dims: pltpu.VMEM(dims, BF16)
    count = probes.shape[1]
    out, answer, residual, m0, vf, uf, af, r0, w = pl.pallas_call(
        functools.partial(exchange_kernel, sizes),
        out_shape=(
            shape(PANEL, tile),
            shape(count // n_c, PANEL),
            shape(1),
            shape(CHUNKS, PANEL, PANEL),
            shape(CHUNKS, wide, PANEL),
            shape(PANEL, wide),
            shape(wide, wide),
            shape(count // n_c, PANEL),
            shape(wide, count // n_y),
        ),
        in_specs=[ANY] * 6,
        out_specs=(VMEM, VMEM, SMEM) + (ANY,) * 4 + (VMEM,) * 2,
        scratch_shapes=[
            bf16(coupling.shape[0], CHUNKS, PANEL, tile),
            pltpu.SMEM(radial.shape, F32),
            f32(energies.shape[0] // 128, 128),
            i32(labels.shape[0] // 128, 128),
            pltpu.SMEM(pivot_blocks.shape, jnp.int32),
            f32(*probes.shape),
            bf16(CHUNKS, PANEL, count),
            bf16(CHUNKS, PANEL, count),
            f32(CHUNKS, PANEL, PANEL),
            f32(CHUNKS, wide, PANEL),
            f32(PANEL, wide),
            f32(wide, wide),
            f32(wide, wide),
            bf16(wide, wide),
            bf16(wide, wide),
            f32(PANEL, wide),
            f32(2, CHUNKS, PANEL, PANEL),
            f32(CHUNKS, CHUNKS, PANEL, PANEL),
            f32(CHUNKS, tile, PANEL),
            f32(tile // 128, 128, 128),
            f32(CHUNKS, 2, n_t // 2, PANEL, PANEL),
            f32(CHUNKS, 2, n_r // 2, z_rows, PANEL),
            f32(CHUNKS, 2, z_rows // 2, PANEL),
            f32(CHUNKS, z_rows, PANEL),
            f32(CHUNKS, n_t - 1, z_rows // n_t, PANEL),
            f32(wide, wide),
            f32(PANEL, wide),
            f32(PANEL, wide),
            f32(2, n_y // 2, PANEL // n_y, wide),
            f32(PANEL // n_y, wide),
            f32(n_r - 1, PANEL // n_y // n_r, wide),
            f32(PANEL // n_y // n_r, wide),
            f32(n_t, PANEL // n_y // n_r, wide),
            f32(PANEL, wide),
            f32(PANEL // CORES, wide),
            f32(PANEL // CORES, wide),
            f32(2, n_y // 2, PANEL // CORES // n_y, wide),
            f32(PANEL, count),
            f32(CORES, width, PANEL),
            f32(width, PANEL),
            f32(width, PANEL),
            f32(2, n_y // 2, width // n_y, PANEL),
            f32(n_y, z_rows // n_t, count // n_y),
            f32(n_c - 1, z_rows // n_t, count // n_y),
            f32(n_t, n_r * (z_rows // n_t), count // n_y),
            DMA((5 + CHUNKS,)), DMA((3 + CHUNKS,)),
            DMA((CHUNKS, 2, 3)), DMA((CHUNKS, 2, 3)),
            DMA((CHUNKS, 2, n_r // 2)), DMA((CHUNKS, 2, n_r // 2)),
            DMA((CHUNKS, n_t - 1)), DMA((CHUNKS, n_t - 1)),
            DMA((CHUNKS, n_t - 1)), DMA((CHUNKS, n_t - 1)),
            DMA((CHUNKS, 2, n_r // 2)), DMA((CHUNKS, 2, n_r // 2)),
            DMA((5,)), DMA((5,)),
            DMA((2, 3)), DMA((2, 3)),
            DMA((n_r - 1,)), DMA((n_r - 1,)),
            DMA((n_t - 1,)), DMA((n_t - 1,)),
            DMA((n_r - 1,)), DMA((n_r - 1,)),
            DMA((2, 2)), DMA((2, 2)),
            DMA((2, 3)), DMA((2, 3)),
            DMA((2, 2)), DMA((2, 2)),
            DMA((2, 3)), DMA((2, 3)),
            DMA((n_c - 1,)), DMA((n_c - 1,)),
            DMA((n_r - 1,)), DMA((n_r - 1,)),
            DMA((n_t - 1,)), DMA((n_t - 1,)),
        ],
        compiler_params=pltpu.CompilerParams(
            collective_id=0, has_side_effects=True, vmem_limit_bytes=LIMIT
        ),
        name="exchange",
    )(coupling, radial, energies.reshape(-1, 128), labels.reshape(-1, 128), pivot_blocks, probes)
    return pl.pallas_call(
        functools.partial(repair_kernel, sizes),
        out_shape=(shape(PANEL, tile), shape(count // n_c, PANEL)),
        in_specs=[SMEM, SMEM] + [ANY] * 8,
        out_specs=(ANY, ANY),
        scratch_shapes=[
            f32(wide, wide), f32(PANEL, wide), f32(CHUNKS, wide, PANEL), f32(CHUNKS, PANEL, PANEL),
            f32(count // n_c, PANEL), f32(wide, count // n_y), f32(PANEL, tile), f32(count // n_c, PANEL),
            f32(wide, wide), f32(PANEL, wide), f32(CHUNKS, PANEL, PANEL), DMA, DMA((2, CHUNKS + 1)),
        ],
        compiler_params=pltpu.CompilerParams(vmem_limit_bytes=LIMIT),
        name="repair",
    )(residual, pivot_blocks, af, uf, vf, m0, r0, w, out, answer)


def solution(mesh):
    sizes = tuple(mesh.shape[name] for name in ("term", "row", "col"))
    return jax.shard_map(
        functools.partial(on_device, sizes),
        mesh=mesh,
        in_specs=(P("term", "row", "col"), P(), P(), P(), P(), P("col", None)),
        out_specs=(P(("row", "term"), "col"), P("col", ("row", "term"))),
        check_vma=False,
    )
```

```python
import functools

import jax
import jax.numpy as jnp
from jax import lax
from jax.experimental import pallas as pl
from jax.experimental.pallas import tpu as pltpu
from jax.sharding import PartitionSpec as P

MESH = pl.DeviceIdType.MESH
PANEL = 256
CHUNKS = 4
CORES = 2
F32 = jnp.float32
BF16 = jnp.bfloat16
STEP = 0.25


def aligned(index, step):
    return pl.multiple_of(index, step)


class Sends:
    def __init__(self):
        self.copies = []

    def start(self, source, target, send_sem, recv_sem, device):
        copy = pltpu.make_async_remote_copy(
            src_ref=source,
            dst_ref=target,
            send_sem=send_sem,
            recv_sem=recv_sem,
            device_id=device,
            device_id_type=MESH,
        )
        copy.start()
        self.copies.append(copy)
        return copy

    def drain(self):
        for copy in self.copies:
            copy.wait_send()
        self.copies = []


class RingReduce:
    def __init__(self, sends, device_at, pos, n, rows, own, slots, send_sem, recv_sem, source=None, stage=None):
        self.sends, self.device_at, self.pos, self.n, self.rows = sends, device_at, pos, n, rows
        self.own, self.slots, self.send_sem, self.recv_sem = own, slots, send_sem, recv_sem
        self.source, self.stage = source, stage
        self.half = rows // 2
        self.reach = n // 2
        self.sent = {}

    def neighbour(self, way):
        return self.device_at(lax.rem(self.pos + (1 if way == 0 else self.n - 1), self.n))

    def dest(self, way, distance):
        return lax.rem(self.pos + (distance if way == 0 else self.n - distance), self.n)

    def send(self, way, key, source, target):
        self.sent[way, key] = self.sends.start(
            source, target, self.send_sem.at[way, key], self.recv_sem.at[way, key], self.neighbour(way)
        )

    def start(self):
        half = self.half
        for way in range(2):
            dest = self.dest(way, self.reach)
            low = way * half
            if self.source is not None:
                source = self.source.at[pl.ds(aligned(dest * self.rows + low, half), half)]
            else:
                self.stage[way] = self.own(dest, low, half)
                source = self.stage.at[way]
            self.send(way, 0, source, self.slots.at[way, 0, pl.ds(low, half)])
        if self.source is not None:
            for way in range(2):
                dest = self.dest(way, self.reach - 1)
                other = (1 - way) * half
                source = self.source.at[pl.ds(aligned(dest * self.rows + other, half), half)]
                self.send(way, self.reach, source, self.slots.at[way, 1, pl.ds(other, half)])

    def step(self, s):
        half = self.half
        for way in range(2):
            self.sent[way, s - 1].wait_recv()
            dest = self.dest(way, self.reach - s)
            low, other = way * half, (1 - way) * half
            if s == 1:
                self.slots[way, 0, low : low + half] += self.own(dest, low, half)
                if self.source is not None:
                    part = pl.ds(low, half)
                    self.send(way, 1, self.slots.at[way, 0, part], self.slots.at[way, 1, part])
                    continue
                self.slots[way, 0, other : other + half] = self.own(dest, other, half)
            else:
                self.slots[way, s - 1] += self.own(dest, 0, self.rows)
            self.send(way, s, self.slots.at[way, s - 1], self.slots.at[way, s])

    def finish(self):
        for way in range(2):
            self.sent[way, self.reach - 1].wait_recv()
            if self.source is not None:
                self.sent[way, self.reach].wait_recv()
        last = self.reach - 1
        return self.own(self.pos, 0, self.rows) + (self.slots[0, last] + self.slots[1, last])


class RingGather:
    def __init__(self, sends, device_at, pos, n, rows, ref, base, send_sem, recv_sem):
        self.sends, self.device_at, self.pos, self.n, self.rows = sends, device_at, pos, n, rows
        self.ref, self.base, self.send_sem, self.recv_sem = ref, base, send_sem, recv_sem
        self.reach = n // 2
        self.sent = {}

    def step(self, s):
        n = self.n
        for way in range(2):
            if s > 0:
                self.sent[way, s - 1].wait_recv()
            block = lax.rem(self.pos + (n - s if way == 0 else s), n)
            to = self.device_at(lax.rem(self.pos + (1 if way == 0 else n - 1), n))
            rows = self.rows if s < self.reach - 1 else self.rows // 2
            low = 0 if s < self.reach - 1 else way * rows
            part = self.ref.at[pl.ds(aligned(self.base + block * self.rows + low, rows), rows)]
            self.sent[way, s] = self.sends.start(part, part, self.send_sem.at[way, s], self.recv_sem.at[way, s], to)

    def finish(self):
        for way in range(2):
            self.sent[way, self.reach - 1].wait_recv()


def chunk_order(pivots, col):
    first, second = pivots[0], pivots[1]
    own_first = first // CHUNKS == col
    own_second = second // CHUNKS == col
    local_first, local_second = lax.rem(first, CHUNKS), lax.rem(second, CHUNKS)
    lead = jnp.where(own_first, local_first, jnp.where(own_second, local_second, 0))
    order = [lead] + [jnp.where(lead == i, 0, i) for i in range(1, CHUNKS)]
    both = own_first & own_second
    next_up = order[1]
    for i in range(2, CHUNKS):
        order[i] = jnp.where(both & (order[i] == local_second), next_up, order[i])
    order[1] = jnp.where(both, local_second, order[1])
    return order, own_first, own_second


def exchange_kernel(
    sizes, coupling_in, radial_in, energies_in, labels_in, pivots_in, probes_in,
    out, answer, left_out, m0_out, vf_out, uf_out, af_out, r0, w,
    coupling, radial, energies, labels, pivots, probes, p_high, p_low, m0, vf, uf, af, x_ref, a_high, a_low, l_ref,
    vsrc, qn, q, parity, x_slots, z_slots, z_stage, z_mine, z_parts, am, ac, ah, a_slots, a_mine, az, ax_mine, ax,
    um, uc, uh, u_slots, reply, part, r_half, r_got, r_slots, w_mine, w_slots, w_all,
    in_s, out_s,
    x_ss, x_rs, z_ss, z_rs, zx_ss, zx_rs, zg_ss, zg_rs, zy_ss, zy_rs,
    c_ss, c_rs, ay_ss, ay_rs, az_ss, az_rs, ax_ss, ax_rs, ag_ss, ag_rs, ayg_ss, ayg_rs,
    uy_ss, uy_rs, uyg_ss, uyg_rs, ry_ss, ry_rs, wc_ss, wc_rs, wz_ss, wz_rs, wx_ss, wx_rs,
):
    n_t, n_r, n_c = sizes
    n_y = n_c // CORES
    t, z, col = lax.axis_index("term"), lax.axis_index("row"), lax.axis_index("col")
    y, core = col // CORES, lax.rem(col, CORES)
    sends = Sends()
    loads = [
        pltpu.make_async_copy(source, target, in_s.at[i])
        for i, (source, target) in enumerate(
            [(pivots_in, pivots), (radial_in, radial), (labels_in, labels), (energies_in, energies)]
        )
    ]
    blocks = [
        pltpu.make_async_copy(
            coupling_in.at[:, pl.ds(i * PANEL, PANEL)], coupling.at[:, i], in_s.at[4 + i]
        )
        for i in range(CHUNKS)
    ]
    trials = pltpu.make_async_copy(probes_in, probes, in_s.at[4 + CHUNKS])
    for copy in loads + blocks:
        copy.start()

    def at_x(p):
        return {"term": p}

    def at_z(p):
        return {"row": p}

    def at_y(p):
        return {"col": p * CORES + core}

    other_core = {"col": y * CORES + (1 - core)}
    greet = [at_x(lax.rem(t + d, n_t)) for d in range(1, n_t)]
    greet += [at_z(lax.rem(z + d, n_r)) for d in range(1, n_r)]
    greet += [{"col": lax.rem(col + d, n_c)} for d in range(1, n_c)]
    barrier = pltpu.get_barrier_semaphore()
    for device in greet:
        pl.semaphore_signal(barrier, inc=1, device_id=device, device_id_type=MESH)

    for copy in loads:
        copy.wait()
    order, own_first, own_second = chunk_order(pivots, col)
    own_both = own_first & own_second
    piv = (pivots[0], pivots[1])
    col_owned = (own_first, own_second)
    col_chunk = (jnp.int32(0), jnp.where(own_first, 1, 0))

    lab = labels[pl.ds(aligned(z * 8, 8), 8), :]
    lab = lax.rem(lab, 2).astype(F32)
    for b in range(8):
        parity[b] = jnp.broadcast_to(lab[b : b + 1, :], (128, 128)).T

    even = radial[2 * t] * STEP
    odd = radial[2 * t + 1] * STEP
    on_diagonal = jnp.where((z == col) & (t == 0), 1.0, 0.0).astype(F32)

    def column_rows(table, block):
        return [table[pl.ds(col * 8 + block * 2 + i, 1), :] for i in range(2)]

    def layers(group, half, rows, block, col_par, i):
        cols = slice(block * PANEL + i * 128, block * PANEL + (i + 1) * 128)
        c0 = coupling[0, group, rows, cols].astype(F32) * even
        c1 = coupling[1, group, rows, cols].astype(F32) * odd
        return jnp.where(parity[group * 2 + half] == col_par[i], c0, c1)

    same = lax.broadcasted_iota(jnp.int32, (128, 128), 0) == lax.broadcasted_iota(jnp.int32, (128, 128), 1)

    def fill_pivot(k):
        group = lax.rem(piv[k], CHUNKS)
        mine = piv[k] // CHUNKS == z
        for block in range(CHUNKS):
            col_par = [lax.rem(v, 2).astype(F32) for v in column_rows(labels, block)]
            diag = [(1.0 + STEP * v) * on_diagonal for v in column_rows(energies, block)]
            for half in range(2):
                rows = slice(half * 128, (half + 1) * 128)
                for i in range(2):
                    value = layers(group, half, rows, block, col_par, i)
                    if i == half:
                        value = value + jnp.where(same & (group == block), diag[i], 0.0)
                    vsrc[k, block, rows, i * 128 : (i + 1) * 128] = jnp.where(mine, value, 0.0)

    def fill(block):
        col_par = [lax.rem(v, 2).astype(F32) for v in column_rows(labels, block)]

        def body(group, carry):
            for half in range(2):
                rows = slice(half * 128, (half + 1) * 128)
                for i in range(2):
                    qn[block, group, rows, i * 128 : (i + 1) * 128] = layers(group, half, rows, block, col_par, i)
            return carry

        lax.fori_loop(0, CHUNKS, body, 0)
        for i, v in enumerate(column_rows(energies, block)):
            part = slice(i * 128, (i + 1) * 128)
            qn[block, block, part, part] += jnp.where(same, (1.0 + STEP * v) * on_diagonal, 0.0)

    def take(chunk):
        for i in range(CHUNKS):
            q[chunk, i * PANEL : (i + 1) * PANEL, :] = qn[order[chunk], i]

    def x_own(chunk):
        return lambda dest, low, n: q[chunk, pl.ds(aligned(dest * PANEL + low, 128), n), :]

    xr = [
        RingReduce(
            sends, at_x, t, n_t, PANEL, x_own(i), x_slots.at[i], x_ss.at[i], x_rs.at[i], source=q.at[i]
        )
        for i in range(CHUNKS)
    ]

    def x_finish(i):
        m0[i] = xr[i].finish()

    z_rows = 2 * PANEL // n_r

    def z_own(h):
        def load(dest, low, n):
            per = PANEL // z_rows
            which = jnp.where(dest < per, 0, 1)
            return vsrc[which, h, pl.ds(aligned(lax.rem(dest, per) * z_rows + low, 32), n), :]

        return load

    zr = [
        RingReduce(
            sends, at_z, z, n_r, z_rows, z_own(h), z_slots.at[h], z_ss.at[h], z_rs.at[h], stage=z_stage.at[h]
        )
        for h in range(CHUNKS)
    ]
    zg = [
        RingGather(sends, at_z, z, n_r, z_rows, vf.at[h], 0, zy_ss.at[h], zy_rs.at[h]) for h in range(CHUNKS)
    ]
    piece = z_rows // n_t
    zx = [{} for _ in range(CHUNKS)]
    zxg = [{} for _ in range(CHUNKS)]

    def z_finish(h):
        z_mine[h] = zr[h].finish()
        for d in range(1, n_t):
            dest = lax.rem(t + d, n_t)
            zx[h][d] = sends.start(
                z_mine.at[h, pl.ds(aligned(dest * piece, piece), piece)],
                z_parts.at[h, d - 1],
                zx_ss.at[h, d - 1],
                zx_rs.at[h, d - 1],
                at_x(dest),
            )

    def z_sum(h):
        for d in range(1, n_t):
            zx[h][d].wait_recv()
        total = z_mine[h, pl.ds(aligned(t * piece, piece), piece), :]
        for d in range(1, n_t):
            total = total + z_parts[h, d - 1]
        mine = pl.ds(aligned(z * z_rows + t * piece, piece), piece)
        vf[h, mine, :] = total
        for d in range(1, n_t):
            dest = lax.rem(t + d, n_t)
            zxg[h][d] = sends.start(
                vf.at[h, mine], vf.at[h, mine], zg_ss.at[h, d - 1], zg_rs.at[h, d - 1], at_x(dest)
            )

    def z_gather(h, s):
        if s == 0:
            for d in range(1, n_t):
                zxg[h][d].wait_recv()
        zg[h].step(s)

    def a_load():
        for k in range(2):
            for l in range(2):
                am[k * PANEL : (k + 1) * PANEL, l * PANEL : (l + 1) * PANEL] = jnp.where(
                    col_owned[l], vsrc[k, lax.rem(piv[l], CHUNKS)], 0.0
                )

    a_ring = RingReduce(
        sends, at_y, y, n_y, PANEL // n_y,
        lambda dest, low, n: ah[pl.ds(aligned(dest * (PANEL // n_y) + low, 32), n), :],
        a_slots, ay_ss, ay_rs, source=ah,
    )
    a_state = {}

    def a_core():
        a_load()
        a_state["core"] = sends.start(
            am.at[pl.ds(aligned((1 - core) * PANEL, PANEL), PANEL)], ac, c_ss.at[0], c_rs.at[0], other_core
        )

    def a_y0():
        a_state["core"].wait_recv()
        ah[...] = am[pl.ds(aligned(core * PANEL, PANEL), PANEL), :] + ac[...]
        a_ring.start()

    def a_y1():
        a_ring.step(1)

    a_rows = PANEL // n_y
    a_piece = a_rows // n_r

    def a_z():
        a_mine[...] = a_ring.finish()
        a_state["z"] = []
        for d in range(1, n_r):
            dest = lax.rem(z + d, n_r)
            a_state["z"].append(
                sends.start(
                    a_mine.at[pl.ds(aligned(dest * a_piece, a_piece), a_piece)],
                    az.at[d - 1],
                    az_ss.at[d - 1],
                    az_rs.at[d - 1],
                    at_z(dest),
                )
            )

    def a_x():
        for copy in a_state["z"]:
            copy.wait_recv()
        total = a_mine[pl.ds(aligned(z * a_piece, a_piece), a_piece), :]
        for d in range(1, n_r):
            total = total + az[d - 1]
        ax_mine[...] = total
        ax[t] = total
        a_state["x"] = []
        for d in range(1, n_t):
            a_state["x"].append(
                sends.start(ax_mine, ax.at[t], ax_ss.at[d - 1], ax_rs.at[d - 1], at_x(lax.rem(t + d, n_t)))
            )

    def a_back():
        for copy in a_state["x"]:
            copy.wait_recv()
        total = ax[0]
        for d in range(1, n_t):
            total = total + ax[d]
        mine = pl.ds(aligned(core * PANEL + y * a_rows + z * a_piece, a_piece), a_piece)
        af[mine, :] = total
        a_state["zg"] = [
            sends.start(
                af.at[mine], af.at[mine], ag_ss.at[d - 1], ag_rs.at[d - 1], at_z(lax.rem(z + d, n_r))
            )
            for d in range(1, n_r)
        ]

    a_gather = RingGather(sends, at_y, y, n_y, a_rows, af, core * PANEL, ayg_ss, ayg_rs)

    def a_yg0():
        for copy in a_state["zg"]:
            copy.wait_recv()
        a_gather.step(0)

    def a_yg1():
        a_gather.step(1)

    def a_core_back():
        a_gather.finish()
        part = af.at[pl.ds(aligned(core * PANEL, PANEL), PANEL)]
        a_state["core"] = sends.start(part, part, c_ss.at[1], c_rs.at[1], other_core)

    def a_done():
        a_state["core"].wait_recv()

    u_half = PANEL // CORES
    u_rows = u_half // n_y
    u_ring = RingReduce(
        sends, at_y, y, n_y, u_rows,
        lambda dest, low, n: uh[pl.ds(aligned(dest * u_rows + low, 16), n), :],
        u_slots, uy_ss, uy_rs, source=uh,
    )
    u_gather = RingGather(sends, at_y, y, n_y, u_rows, uf, core * u_half, uyg_ss, uyg_rs)
    u_state = {}

    def u_core():
        for l in range(2):
            um[:, l * PANEL : (l + 1) * PANEL] = jnp.where(col_owned[l], m0[col_chunk[l]], 0.0)
        u_state["core"] = sends.start(
            um.at[pl.ds(aligned((1 - core) * u_half, u_half), u_half)], uc, c_ss.at[2], c_rs.at[2], other_core
        )

    def u_y0():
        u_state["core"].wait_recv()
        uh[...] = um[pl.ds(aligned(core * u_half, u_half), u_half), :] + uc[...]
        u_ring.start()

    def u_y1():
        u_ring.step(1)

    def u_yg0():
        uf[pl.ds(aligned(core * u_half + y * u_rows, u_rows), u_rows), :] = u_ring.finish()
        u_gather.step(0)

    def u_yg1():
        u_gather.step(1)

    def u_core_back():
        u_gather.finish()
        part = uf.at[pl.ds(aligned(core * u_half, u_half), u_half)]
        u_state["core"] = sends.start(part, part, c_ss.at[3], c_rs.at[3], other_core)

    def u_done():
        u_state["core"].wait_recv()

    n = 2 * PANEL
    eye = lambda: jnp.where(
        lax.broadcasted_iota(jnp.int32, (n, n), 0) == lax.broadcasted_iota(jnp.int32, (n, n), 1), 1.0, 0.0
    ).astype(F32)
    stores = []

    def store(source, target):
        copy = pltpu.make_async_copy(source, target, out_s.at[len(stores)])
        copy.start()
        stores.append(copy)

    def split_trials():
        trials.wait()
        for i in range(CHUNKS):
            p_high[i], p_low[i] = split(probes[i * PANEL : (i + 1) * PANEL, :])

    def inv_start():
        store(af, af_out)
        high, low = split(af[...])
        a_high[...], a_low[...] = high, low
        square = dot(high, high, (((0,), (0,)), ((), ())))
        x_ref[...] = af[...].T * (1.8 / jnp.max(jnp.sum(jnp.abs(square), axis=0, keepdims=True)))

    def coarse(count):
        def body(i, carry):
            x = x_ref[...]
            high = x.astype(BF16)
            rest = eye() - dot(a_high[...], high)
            x_ref[...] = x + dot(high, rest.astype(BF16))
            return carry

        lax.fori_loop(0, count, body, 0)

    def fine():
        x = x_ref[...]
        x_parts = split(x)
        rest = eye() - dot3((a_high[...], a_low[...]), x_parts)
        x_ref[...] = x + dot(x_parts[0], rest.astype(BF16))
        return jnp.sum(rest * rest)

    group = z * n_t + t
    is_first, is_second = group == piv[0], group == piv[1]
    keep = jnp.where(is_first | is_second, 0.0, 1.0).astype(F32)
    state = {}

    def inv_end():
        left_out[0] = fine()
        x = x_ref[...]
        factor = dot3(split(uf[...]), split(x))
        factor = jnp.where(is_first, -x[:PANEL, :], jnp.where(is_second, -x[PANEL:, :], factor))
        l_ref[...] = factor
        state["left"] = split(factor)

    def update(block):
        where = jnp.int32(0)
        for chunk in range(1, CHUNKS):
            where = jnp.where(order[chunk] == block, chunk, where)
        value = m0[where] * keep - dot3(state["left"], split(vf[block]))
        for l in range(2):
            here = col_owned[l] & (lax.rem(piv[l], CHUNKS) == block)
            value = jnp.where(here, -l_ref[:, l * PANEL : (l + 1) * PANEL], value)
        out[:, block * PANEL : (block + 1) * PANEL] = value

    def r_add(chunk):
        factor = keep
        if chunk == 0:
            factor = jnp.where(own_first | own_second, 0.0, keep)
        if chunk == 1:
            factor = jnp.where(own_both, 0.0, keep)
        add = dot3(split(m0[chunk] * factor), (p_high[order[chunk]], p_low[order[chunk]]))
        if chunk == 0:
            reply[...] = add
        else:
            reply[...] += add

    r_rows = part.shape[1] // n_y
    r_ring = RingReduce(
        sends, at_y, y, n_y, r_rows,
        lambda dest, low, n: r_half[pl.ds(aligned(dest * r_rows + low, 32), n), :],
        r_slots, ry_ss, ry_rs, source=r_half,
    )

    def r_core():
        turned = reply[...].T
        for j in range(n_c):
            part[j % CORES, (j // CORES) * r_rows : (j // CORES + 1) * r_rows, :] = turned[
                j * r_rows : (j + 1) * r_rows, :
            ]
        state["r"] = sends.start(part.at[1 - core], r_got, c_ss.at[4], c_rs.at[4], other_core)

    def r_y0():
        state["r"].wait_recv()
        r_half[...] = part[core] + r_got[...]
        r_ring.start()

    def r_y1():
        r_ring.step(1)

    def r_done():
        r0[...] = r_ring.finish()

    lanes = w_mine.shape[2]

    def w_cols():
        first = z * z_rows + t * piece
        row_id = lax.broadcasted_iota(jnp.int32, (piece, PANEL), 0) + first
        col_id = lax.broadcasted_iota(jnp.int32, (piece, PANEL), 1)
        total = jnp.zeros((piece, probes.shape[1]), F32)
        for h in range(CHUNKS):
            value = vf[h, pl.ds(aligned(first, piece), piece), :]
            for l in range(2):
                here = col_owned[l] & (lax.rem(piv[l], CHUNKS) == h)
                unit = jnp.where(row_id == col_id + l * PANEL, 1.0, 0.0).astype(F32)
                value = jnp.where(here, unit, value)
            total = total + dot3(split(value), (p_high[h], p_low[h]))
        for i in range(n_y):
            w_mine[i] = total[:, i * lanes : (i + 1) * lanes]
        state["wc"] = []
        for d in range(1, n_c):
            dest = lax.rem(col + d, n_c)
            state["wc"].append(
                sends.start(
                    w_mine.at[dest // CORES], w_slots.at[d - 1], wc_ss.at[d - 1], wc_rs.at[d - 1], {"col": dest}
                )
            )

    def w_z():
        total = w_mine[y]
        for d in range(1, n_c):
            state["wc"][d - 1].wait_recv()
            total = total + w_slots[d - 1]
        mine = pl.ds(aligned(z * piece, piece), piece)
        w_all[t, mine, :] = total
        state["wz"] = [
            sends.start(
                w_all.at[t, mine], w_all.at[t, mine], wz_ss.at[d - 1], wz_rs.at[d - 1], at_z(lax.rem(z + d, n_r))
            )
            for d in range(1, n_r)
        ]

    def w_x():
        for copy in state["wz"]:
            copy.wait_recv()
        state["wx"] = [
            sends.start(w_all.at[t], w_all.at[t], wx_ss.at[d - 1], wx_rs.at[d - 1], at_x(lax.rem(t + d, n_t)))
            for d in range(1, n_t)
        ]

    def w_done():
        for copy in state["wx"]:
            copy.wait_recv()
        for i in range(n_t):
            for j in range(n_r):
                first = j * z_rows + i * piece
                w[first : first + piece, :] = w_all[i, j * piece : (j + 1) * piece, :]

    def respond():
        both = dot3(state["left"], split(w[...])).T
        answer[...] = r0[...] - jnp.where(core == 0, both[:r_rows], both[r_rows:])

    for copy in blocks:
        copy.wait()
    fill_pivot(0)
    fill_pivot(1)
    pl.semaphore_wait(barrier, len(greet))
    for i in range(CHUNKS):
        zr[i].start()
    a_core()
    trials.start()
    for i in range(CHUNKS):
        fill(i)
    take(0)
    xr[0].start()
    for i in range(CHUNKS):
        zr[i].step(1)
    a_y0()
    take(1)
    take(2)
    take(3)
    for i in (0, 1):
        zr[i].step(2)
    xr[0].step(1)
    xr[1].start()
    a_y1()
    for i in (2, 3):
        zr[i].step(2)
    split_trials()
    a_z()
    for i in (0, 1):
        zr[i].step(3)
    x_finish(0)
    a_x()
    for i in (2, 3):
        zr[i].step(3)
    xr[1].step(1)
    xr[2].start()
    a_back()
    for i in (0, 1):
        z_finish(i)
    a_yg0()
    for i in (2, 3):
        z_finish(i)
    x_finish(1)
    u_core()
    r_add(0)
    r_add(1)
    for i in (0, 1):
        z_sum(i)
    a_yg1()
    for i in (2, 3):
        z_sum(i)
    xr[2].step(1)
    xr[3].start()
    u_y0()
    for i in (0, 1):
        z_gather(i, 0)
    a_core_back()
    for i in (2, 3):
        z_gather(i, 0)
    w_cols()
    u_y1()
    for i in (0, 1):
        z_gather(i, 1)
    x_finish(2)
    xr[3].step(1)
    u_yg0()
    for i in (2, 3):
        z_gather(i, 1)
    a_done()
    inv_start()
    coarse(2)
    w_z()
    u_yg1()
    r_add(2)
    coarse(2)
    for i in (0, 1):
        z_gather(i, 2)
    for i in (2, 3):
        z_gather(i, 2)
    x_finish(3)
    r_add(3)
    r_core()
    w_x()
    u_core_back()
    coarse(4)
    store(m0, m0_out)
    for i in (0, 1):
        z_gather(i, 3)
    r_y0()
    for i in (2, 3):
        z_gather(i, 3)
    u_done()
    store(uf, uf_out)
    r_y1()
    fine()
    w_done()
    inv_end()
    zg[0].finish()
    store(vf.at[0], vf_out.at[0])
    update(0)
    zg[1].finish()
    store(vf.at[1], vf_out.at[1])
    update(1)
    zg[2].finish()
    store(vf.at[2], vf_out.at[2])
    update(2)
    zg[3].finish()
    store(vf.at[3], vf_out.at[3])
    update(3)
    r_done()
    respond()
    for copy in stores:
        copy.wait()
    sends.drain()


def split(value):
    high = value.astype(BF16)
    return high, (value - high.astype(F32)).astype(BF16)


def dot(a, b, dims=(((1,), (0,)), ((), ()))):
    return lax.dot_general(a, b, dims, preferred_element_type=F32)


def dot3(a, b, dims=(((1,), (0,)), ((), ()))):
    return dot(a[0], b[0], dims) + (dot(a[0], b[1], dims) + dot(a[1], b[0], dims))


def invert(af, x_ref):
    n = 2 * PANEL
    a = af[...]
    eye = jnp.where(
        lax.broadcasted_iota(jnp.int32, (n, n), 0) == lax.broadcasted_iota(jnp.int32, (n, n), 1), 1.0, 0.0
    ).astype(F32)
    size = jnp.abs(a)
    scale = 1.0 / (jnp.max(jnp.sum(size, axis=0, keepdims=True)) * jnp.max(jnp.sum(size, axis=1, keepdims=True)))
    a_high, a_low = split(a)
    x_ref[...] = a.T * scale

    def coarse(state):
        count, _ = state
        x = x_ref[...]
        x_high = x.astype(BF16)
        rest = eye - dot(a_high, x_high)
        x_ref[...] = x + dot(x_high, rest.astype(BF16))
        return count + 1, jnp.sum(rest * rest)

    _, left = lax.while_loop(lambda s: (s[0] < 24) & (s[1] > 0.1), coarse, (jnp.int32(0), jnp.float32(1e9)))

    def fine(state):
        count, _ = state
        x = x_ref[...]
        x_parts = split(x)
        rest = eye - dot3((a_high, a_low), x_parts)
        x_ref[...] = x + dot3(x_parts, split(rest))
        return count + 1, jnp.sum(rest * rest)

    start = jnp.where(left < 0.5, 0, 100).astype(jnp.int32)
    count, left = lax.while_loop(lambda s: (s[0] < 6) & (s[1] > 1e-6), fine, (start, jnp.float32(1e9)))

    def exact(a, b):
        return jnp.dot(a, b, precision=lax.Precision.HIGHEST, preferred_element_type=F32)

    @pl.when(left > 1e-6)
    def _():
        x_ref[...] = af[...].T * scale

        def full(state):
            count, _ = state
            x = x_ref[...]
            rest = eye - exact(af[...], x)
            x_ref[...] = x + exact(x, rest)
            return count + 1, jnp.sum(rest * rest)

        lax.while_loop(lambda s: (s[0] < 60) & (s[1] > 1e-7), full, (jnp.int32(0), jnp.float32(1e9)))


def repair_kernel(
    sizes, residual, pivots, af_in, uf_in, vf_in, m0_in, r0_in, w_in, out_old, answer_old, out_new, answer_new,
    af, uf, vf, m0, r0, w, out, answer, x_ref, l_ref, mp, sem, sems,
):
    quarter = PANEL // CHUNKS
    parts = [pl.ds(i * quarter, quarter) for i in range(CHUNKS)]
    pairs = [(out_old.at[p], out.at[p], out_new.at[p]) for p in parts] + [(answer_old, answer, answer_new)]
    moves = [
        (pltpu.make_async_copy(a, b, sems.at[0, i]), pltpu.make_async_copy(b, c, sems.at[1, i]))
        for i, (a, b, c) in enumerate(pairs)
    ]
    for first, _ in moves:
        first.start()
    for first, second in moves:
        first.wait()
        second.start()
    for _, second in moves:
        second.wait()

    @pl.when(~(residual[0] < 1e-5))
    def _():
        for source, target in [(af_in, af), (uf_in, uf), (vf_in, vf), (m0_in, m0), (r0_in, r0), (w_in, w)]:
            copy = pltpu.make_async_copy(source, target, sem)
            copy.start()
            copy.wait()
        n_t, n_r, n_c = sizes
        t, z, col = lax.axis_index("term"), lax.axis_index("row"), lax.axis_index("col")
        group = z * n_t + t
        order, own_first, own_second = chunk_order(pivots, col)
        own_both = own_first & own_second
        invert(af, x_ref)
        inverse = split(x_ref[...])
        l_ref[...] = dot3(split(uf[...]), inverse)
        is_first, is_second = group == pivots[0], group == pivots[1]

        @pl.when(is_first)
        def _():
            l_ref[...] = -x_ref[:PANEL, :]

        @pl.when(is_second)
        def _():
            l_ref[...] = -x_ref[PANEL:, :]

        keep = jnp.where(is_first | is_second, 0.0, 1.0).astype(F32)
        left = split(l_ref[...])
        for chunk in range(CHUNKS):
            rows = vf[order[chunk]]
            value = m0[chunk] * keep - dot3(left, split(rows))
            if chunk == 0:
                value = jnp.where(
                    own_first, -l_ref[:, :PANEL], jnp.where(own_second, -l_ref[:, PANEL:], value)
                )
            if chunk == 1:
                value = jnp.where(own_both, -l_ref[:, PANEL:], value)
            mp[chunk] = value
        for block in range(CHUNKS):
            where = jnp.int32(0)
            for chunk in range(1, CHUNKS):
                where = jnp.where(order[chunk] == block, chunk, where)
            out[:, block * PANEL : (block + 1) * PANEL] = mp[where]
        both = dot3(left, split(w[...])).T
        rows = answer.shape[0]
        answer[...] = r0[...] - jnp.where(lax.rem(col, CORES) == 0, both[:rows], both[rows:])
        for source, target in [(out, out_new), (answer, answer_new)]:
            copy = pltpu.make_async_copy(source, target, sem)
            copy.start()
            copy.wait()


VMEM = pl.BlockSpec(memory_space=pltpu.VMEM)
SMEM = pl.BlockSpec(memory_space=pltpu.SMEM)
ANY = pl.BlockSpec(memory_space=pl.ANY)
LIMIT = 63 * 1024 * 1024
DMA = pltpu.SemaphoreType.DMA


def on_device(sizes, coupling, radial, energies, labels, pivot_blocks, probes):
    n_t, n_r, n_c = sizes
    n_y = n_c // CORES
    tile = coupling.shape[1]
    wide = 2 * PANEL
    z_rows = wide // n_r
    f32 = lambda *shape: pltpu.VMEM(shape, F32)
    width = probes.shape[1] // CORES
    shape = lambda *dims: jax.ShapeDtypeStruct(dims, F32)
    i32 = lambda *dims: pltpu.VMEM(dims, jnp.int32)
    bf16 = lambda *dims: pltpu.VMEM(dims, BF16)
    count = probes.shape[1]
    out, answer, residual, m0, vf, uf, af, r0, w = pl.pallas_call(
        functools.partial(exchange_kernel, sizes),
        out_shape=(
            shape(PANEL, tile),
            shape(count // n_c, PANEL),
            shape(1),
            shape(CHUNKS, PANEL, PANEL),
            shape(CHUNKS, wide, PANEL),
            shape(PANEL, wide),
            shape(wide, wide),
            shape(count // n_c, PANEL),
            shape(wide, count // n_y),
        ),
        in_specs=[ANY] * 6,
        out_specs=(VMEM, VMEM, SMEM) + (ANY,) * 4 + (VMEM,) * 2,
        scratch_shapes=[
            bf16(coupling.shape[0], CHUNKS, PANEL, tile),
            pltpu.SMEM(radial.shape, F32),
            f32(energies.shape[0] // 128, 128),
            i32(labels.shape[0] // 128, 128),
            pltpu.SMEM(pivot_blocks.shape, jnp.int32),
            f32(*probes.shape),
            bf16(CHUNKS, PANEL, count),
            bf16(CHUNKS, PANEL, count),
            f32(CHUNKS, PANEL, PANEL),
            f32(CHUNKS, wide, PANEL),
            f32(PANEL, wide),
            f32(wide, wide),
            f32(wide, wide),
            bf16(wide, wide),
            bf16(wide, wide),
            f32(PANEL, wide),
            f32(2, CHUNKS, PANEL, PANEL),
            f32(CHUNKS, CHUNKS, PANEL, PANEL),
            f32(CHUNKS, tile, PANEL),
            f32(tile // 128, 128, 128),
            f32(CHUNKS, 2, n_t // 2, PANEL, PANEL),
            f32(CHUNKS, 2, n_r // 2, z_rows, PANEL),
            f32(CHUNKS, 2, z_rows // 2, PANEL),
            f32(CHUNKS, z_rows, PANEL),
            f32(CHUNKS, n_t - 1, z_rows // n_t, PANEL),
            f32(wide, wide),
            f32(PANEL, wide),
            f32(PANEL, wide),
            f32(2, n_y // 2, PANEL // n_y, wide),
            f32(PANEL // n_y, wide),
            f32(n_r - 1, PANEL // n_y // n_r, wide),
            f32(PANEL // n_y // n_r, wide),
            f32(n_t, PANEL // n_y // n_r, wide),
            f32(PANEL, wide),
            f32(PANEL // CORES, wide),
            f32(PANEL // CORES, wide),
            f32(2, n_y // 2, PANEL // CORES // n_y, wide),
            f32(PANEL, count),
            f32(CORES, width, PANEL),
            f32(width, PANEL),
            f32(width, PANEL),
            f32(2, n_y // 2, width // n_y, PANEL),
            f32(n_y, z_rows // n_t, count // n_y),
            f32(n_c - 1, z_rows // n_t, count // n_y),
            f32(n_t, n_r * (z_rows // n_t), count // n_y),
            DMA((5 + CHUNKS,)), DMA((3 + CHUNKS,)),
            DMA((CHUNKS, 2, 3)), DMA((CHUNKS, 2, 3)),
            DMA((CHUNKS, 2, n_r // 2)), DMA((CHUNKS, 2, n_r // 2)),
            DMA((CHUNKS, n_t - 1)), DMA((CHUNKS, n_t - 1)),
            DMA((CHUNKS, n_t - 1)), DMA((CHUNKS, n_t - 1)),
            DMA((CHUNKS, 2, n_r // 2)), DMA((CHUNKS, 2, n_r // 2)),
            DMA((5,)), DMA((5,)),
            DMA((2, 3)), DMA((2, 3)),
            DMA((n_r - 1,)), DMA((n_r - 1,)),
            DMA((n_t - 1,)), DMA((n_t - 1,)),
            DMA((n_r - 1,)), DMA((n_r - 1,)),
            DMA((2, 2)), DMA((2, 2)),
            DMA((2, 3)), DMA((2, 3)),
            DMA((2, 2)), DMA((2, 2)),
            DMA((2, 3)), DMA((2, 3)),
            DMA((n_c - 1,)), DMA((n_c - 1,)),
            DMA((n_r - 1,)), DMA((n_r - 1,)),
            DMA((n_t - 1,)), DMA((n_t - 1,)),
        ],
        compiler_params=pltpu.CompilerParams(
            collective_id=0, has_side_effects=True, vmem_limit_bytes=LIMIT
        ),
        name="exchange",
    )(coupling, radial, energies.reshape(-1, 128), labels.reshape(-1, 128), pivot_blocks, probes)
    return pl.pallas_call(
        functools.partial(repair_kernel, sizes),
        out_shape=(shape(PANEL, tile), shape(count // n_c, PANEL)),
        in_specs=[SMEM, SMEM] + [ANY] * 8,
        out_specs=(ANY, ANY),
        scratch_shapes=[
            f32(wide, wide), f32(PANEL, wide), f32(CHUNKS, wide, PANEL), f32(CHUNKS, PANEL, PANEL),
            f32(count // n_c, PANEL), f32(wide, count // n_y), f32(PANEL, tile), f32(count // n_c, PANEL),
            f32(wide, wide), f32(PANEL, wide), f32(CHUNKS, PANEL, PANEL), DMA, DMA((2, CHUNKS + 1)),
        ],
        compiler_params=pltpu.CompilerParams(vmem_limit_bytes=LIMIT),
        name="repair",
    )(residual, pivot_blocks, af, uf, vf, m0, r0, w, out, answer)


def solution(mesh):
    sizes = tuple(mesh.shape[name] for name in ("term", "row", "col"))
    return jax.shard_map(
        functools.partial(on_device, sizes),
        mesh=mesh,
        in_specs=(P("term", "row", "col"), P(), P(), P(), P(), P("col", None)),
        out_specs=(P(("row", "term"), "col"), P("col", ("row", "term"))),
        check_vma=False,
    )
```
